512 devices in a mesh: node: 64 (over z, x, core), local: 8 (over y).
Axes of the slice: x: 4, y: 8, z: 8, core: 2. Of those that a mesh axis runs over, the one named last changes fastest.
Arguments:
- input_activation_matrix: bfloat16 [65536, 1024], P(('node', 'local')), may hold values from -6 to 6
- output_adjoint: bfloat16 [65536, 1024], P(('node', 'local')), may hold values from -6 to 6
- dispatch_mixing_factors: bfloat16 [65536, 8], P(('node', 'local')), may hold values from 0.049804688 to 0.59765625
- permitted_machine_sets: int32 [65536, 4], P(('node', 'local')), may hold values from 0 to 63, all different within a row; in each aligned block of 128 rows (0 to 127, 128 to 255, ...) at most 12 rows name the same one
- chosen_machine_specialist_tuples: int32 [65536, 8], P(('node', 'local')), may hold values from 0 to 31, as said below
- quota_per_class: int32 [512], P('node'), may hold values from 24 to 48, as said below
- gating_matrix_tensor: bfloat16 [512, 1024, 512], P(('node', 'local')), may hold values from -0.1875 to 0.1875
- widening_matrix_tensor: bfloat16 [512, 1024, 512], P(('node', 'local')), may hold values from -0.1875 to 0.1875
- shrinking_matrix_tensor: bfloat16 [512, 512, 1024], P(('node', 'local')), may hold values from -0.25 to 0.25
Outputs:
- mixed: bfloat16 [65536, 1024], P(('node', 'local'))
- input_grad: bfloat16 [65536, 1024], P(('node', 'local'))
- coefficient_derivative: bfloat16 [65536, 8], P(('node', 'local'))
The draws below stay inside these ranges and needn't reach their ends.
Inputs may be any that keep to these rules, and one draw needn't show every extreme that they name: `permitted_machine_sets`: each row names 4 different node groups; in each aligned block of 128 rows (the rows of one device) no group is named by more than 12 rows. `chosen_machine_specialist_tuples`: each row holds 8 different numbers; number c picks position c // 8 of the token's permitted_machine_sets row and expert c mod 8 of that group; each of the 4 positions is picked at least once. `quota_per_class`: each a multiple of 8.
All inputs are finite; a program needn't handle non-finite values.
Results may differ from the reference program's by a relative error of at most 0.018.
Values may be sent and summed in bfloat16 or wider, within the bound.
A program may use at most 64 MiB of HBM per device.

```python
import math
import jax
import jax.numpy as jnp
import numpy as np
from jax import lax

D = 1024
F = 512
TOP = 8
KG = 4
TOK_DEV = 128
EXPERTS = 512
TOKENS = 65536
PAD = 8
LARGEST_QUOTA = 48
CAP = 384
MOST_G = 12
N_NODE = 64
N_LOCAL = 8


def draw_chosen_machine_specialist_tuples(key, part):
    key = jax.random.fold_in(key, 11)
    bias_key, noise_key, order_key = jax.random.split(key, 3)
    code_count = KG * N_LOCAL
    code_ids = jnp.arange(code_count, dtype=jnp.int32)
    local_bias = jax.random.randint(bias_key, (N_LOCAL,), 0, 1024)
    noise_vals = jax.random.randint(noise_key, (TOKENS, code_count), 0, 1024)
    scores = (noise_vals + local_bias[code_ids % N_LOCAL][None, :]) * code_count + code_ids[None, :]
    per_slot = scores.reshape(TOKENS, KG, N_LOCAL)
    top_vals, first_local = lax.top_k(per_slot, 1)
    first_code = jnp.arange(KG, dtype=jnp.int32)[None, :] * N_LOCAL + first_local[:, :, 0].astype(jnp.int32)
    taken_mask = jnp.any(first_code[:, :, None] == code_ids[None, None, :], axis=1)
    rest_scores = jnp.where(taken_mask, -1, scores)
    rest_vals, rest_code = lax.top_k(rest_scores, TOP - KG)
    picked = jnp.concatenate([first_code, rest_code.astype(jnp.int32)], axis=1)
    shuffle_keys = jax.random.randint(order_key, (TOKENS, TOP), 0, 1 << 20) * TOP + jnp.arange(TOP, dtype=jnp.int32)[None, :]
    shuffle_vals, shuffle_order = lax.top_k(shuffle_keys, TOP)
    return jnp.take_along_axis(picked, shuffle_order.astype(jnp.int32), axis=1).astype(jnp.int32)


def draw_quota_per_class(key, part):
    key = jax.random.fold_in(key, 23)
    level_key, fullest_key = jax.random.split(key)
    levels = jax.random.randint(level_key, (N_NODE, N_LOCAL), 3, 7)
    fullest = jax.random.randint(fullest_key, (N_NODE,), 0, N_LOCAL)
    levels = jnp.where(jnp.arange(N_LOCAL)[None, :] == fullest[:, None], 6, levels)
    return (levels * PAD).reshape(-1).astype(jnp.int32)


def level_of(rng, dims, shards, least, high):
    def one(axis_at, shards_of):
        draws = jax.random.uniform(jax.random.fold_in(jax.random.fold_in(rng, 6), axis_at), (shards_of,), jnp.float32, least / len(shards), high / len(shards))
        return jnp.repeat(jnp.exp(draws), dims[axis_at] // shards_of).reshape((-1,) + (1,) * (len(dims) - axis_at - 1))

    level = one(*shards[0])
    for cut in shards[1:]:
        level = level * one(*cut)
    return level


def shared_out(rng, own, number, rows, number_of, top, limit, lean):
    ranking = jax.random.permutation(rng, number_of)
    heavy_load, ordinary = load_shares(number_of, rows * top, limit, lean, True), load_shares(number_of, rows * top, limit, lean, False)
    places = jnp.arange(number_of)

    def named(lengths, turn):
        used = int((lengths > 0).sum())
        fixed = max(1, used // 4)
        passed = fixed + (places - fixed + turn * (used - fixed)) % max(1, number_of - fixed)
        return jnp.zeros((number_of,), jnp.int32).at[ranking[jnp.where(places < fixed, places, passed)]].set(jnp.asarray(lengths, jnp.int32))

    lengths = jnp.where(number % 4 == 0, named(heavy_load, number // 4), named(ordinary, number - number // 4 - 1))
    mixed = jax.random.permutation(jax.random.fold_in(own, 3), number_of)
    giver, receiver = mixed[0:number_of // 2 * 2:2], mixed[1:number_of // 2 * 2:2]
    room = jnp.minimum(lengths[giver] - 1, limit - lengths[receiver]) // 2
    room = jnp.where((giver == ranking[0]) | (receiver == ranking[0]) | (lengths[receiver] == 0), 0, jnp.maximum(room, 0))
    passed = jax.random.randint(jax.random.fold_in(own, 4), (number_of // 2,), 0, 1 << 20) % (room + 1)
    lengths = lengths.at[giver].add(-passed).at[receiver].add(passed)
    items = jnp.searchsorted(jnp.cumsum(lengths), jnp.arange(rows * top), side="right").astype(jnp.int32)
    listing = items.reshape(top, rows).T
    listing = listing[jax.random.permutation(jax.random.fold_in(own, 1), rows)]
    turn = jax.random.randint(jax.random.fold_in(own, 2), (rows, 1), 0, top)
    return jnp.take_along_axis(listing, (jnp.arange(top)[None, :] + turn) % top, axis=1)


def load_shares(count, total, bound, slope, full):
    weights = [(1 << 20) // math.isqrt(standing ** slope) + 1 for standing in range(1, count + 1)]
    largest = bound if full else min(bound, max(-(-total // count), total * weights[0] // sum(weights)))
    least = 1 if total - largest >= count - 1 else 0
    given, spare = [largest] + [least] * (count - 1), total - largest - least * (count - 1)
    while spare > 0:
        free = [i for i in range(1, count) if given[i] < largest] or [i for i in range(1, count) if given[i] < bound]
        mass, budget = sum([weights[i] for i in free]), spare
        for i in free:
            more = min(bound - given[i], max(1, budget * weights[i] // mass), spare)
            given[i] = given[i] + more
            spare = spare - more
    return np.array(given)


def scatter_about(stream_key, shape, scale, limit, cuts=(), kind=jnp.bfloat16):
    array = scale * jax.random.normal(stream_key, shape, jnp.float32)
    if cuts:
        array = array * level_of(stream_key, shape, cuts, -0.22, 0.18)
    return jnp.clip(array, -limit, limit).astype(kind)


def setup_inputs(seed: int = 0) -> dict:
    key_of = jax.random.split(jax.random.key(seed), 10)
    input_activation_matrix = scatter_about(key_of[0], (TOKENS, D), 1.0, 6.0, ((0, 512),))
    output_adjoint = scatter_about(key_of[1], (TOKENS, D), 1.0, 6.0, ((0, 512),))
    dispatch_mixing_factors = jnp.clip(jnp.exp(math.log(0.59765625) - 2.4849066 * jax.random.uniform(key_of[2], (TOKENS, TOP), jnp.float32) ** level_of(key_of[2], (TOKENS, TOP), ((0, 512),), -0.2, 0.2)), 0.049804688, 0.59765625).astype(jnp.bfloat16)
    permitted_machine_sets_keys = jax.random.split(jax.random.fold_in(key_of[3], 1), TOKENS // TOK_DEV)
    permitted_machine_sets_turns = jax.random.permutation(jax.random.fold_in(key_of[3], 3), TOKENS // TOK_DEV)
    permitted_machine_sets = jax.vmap(lambda own, number: shared_out(jax.random.fold_in(key_of[3], 2), own, number, TOK_DEV, N_NODE, KG, MOST_G, 2))(permitted_machine_sets_keys, permitted_machine_sets_turns).reshape((TOKENS, KG))
    chosen_machine_specialist_tuples = draw_chosen_machine_specialist_tuples(jax.random.fold_in(key_of[9], 71), 0)
    quota_per_class = draw_quota_per_class(jax.random.fold_in(key_of[9], 71), 0)
    gating_matrix_tensor = scatter_about(key_of[6], (EXPERTS, D, F), D ** -0.5, 0.1875, ((0, 512),))
    widening_matrix_tensor = scatter_about(key_of[7], (EXPERTS, D, F), D ** -0.5, 0.1875, ((0, 512),))
    shrinking_matrix_tensor = scatter_about(key_of[8], (EXPERTS, F, D), F ** -0.5, 0.25, ((0, 512),))
    return {"input_activation_matrix": input_activation_matrix, "output_adjoint": output_adjoint, "dispatch_mixing_factors": dispatch_mixing_factors, "permitted_machine_sets": permitted_machine_sets, "chosen_machine_specialist_tuples": chosen_machine_specialist_tuples, "quota_per_class": quota_per_class, "gating_matrix_tensor": gating_matrix_tensor, "widening_matrix_tensor": widening_matrix_tensor, "shrinking_matrix_tensor": shrinking_matrix_tensor}


def activations(row_block, weight_gate, weight_up):
    gate_act = jnp.dot(row_block, weight_gate, preferred_element_type=jnp.float32)
    up_act = jnp.dot(row_block, weight_up, preferred_element_type=jnp.float32)
    return gate_act, up_act


def expert_outputs(gate_act, up_act, weight_down):
    sigmoid_act = jax.nn.sigmoid(gate_act)
    hidden = (gate_act * sigmoid_act * up_act).astype(jnp.bfloat16)
    return jnp.dot(hidden, weight_down, preferred_element_type=jnp.float32).astype(jnp.bfloat16)


def contract_last(left_side, right_side):
    return lax.dot_general(left_side, right_side, (((1,), (1,)), ((), ())), preferred_element_type=jnp.float32)


def expert_grads(gate_act, up_act, outputs, gate_vals, upstream, weight_gate, weight_up, weight_down):
    sigmoid_act = jax.nn.sigmoid(gate_act)
    back_prop = gate_vals.astype(jnp.float32)[:, None] * contract_last(upstream, weight_down)
    grad_gate = (back_prop * up_act * sigmoid_act * (1.0 + gate_act * (1.0 - sigmoid_act))).astype(jnp.bfloat16)
    grad_up = (back_prop * gate_act * sigmoid_act).astype(jnp.bfloat16)
    grad_rows = (contract_last(grad_gate, weight_gate) + contract_last(grad_up, weight_up)).astype(jnp.bfloat16)
    grad_weight = jnp.sum(upstream.astype(jnp.float32) * outputs.astype(jnp.float32), axis=1).astype(jnp.bfloat16)
    return grad_rows, grad_weight


def reference(input_activation_matrix, output_adjoint, dispatch_mixing_factors, permitted_machine_sets, chosen_machine_specialist_tuples, quota_per_class, gating_matrix_tensor, widening_matrix_tensor, shrinking_matrix_tensor):
    token_total = input_activation_matrix.shape[0]
    feature = input_activation_matrix.shape[1]
    slot_pick = (chosen_machine_specialist_tuples // N_LOCAL).astype(jnp.int32)
    group_id = jnp.take_along_axis(permitted_machine_sets, slot_pick, axis=1)
    member_ordinal = (group_id * N_LOCAL + chosen_machine_specialist_tuples % N_LOCAL).astype(jnp.int32)
    token_index = jnp.broadcast_to(jnp.arange(token_total, dtype=jnp.int32)[:, None], member_ordinal.shape)
    token_class = (token_index // TOK_DEV) % N_LOCAL
    quota_cell = (member_ordinal * N_LOCAL + token_class).reshape(-1).astype(jnp.int32)
    entries = quota_cell.shape[0]
    sort_order = jnp.argsort(quota_cell, stable=True).astype(jnp.int32)
    counts = jnp.bincount(quota_cell, length=EXPERTS * N_LOCAL).astype(jnp.int32)
    starts = (jnp.cumsum(counts) - counts).astype(jnp.int32)
    sorted_rank = (jnp.arange(entries, dtype=jnp.int32) - starts[quota_cell[sort_order]]).astype(jnp.int32)
    sorting_place = jnp.zeros((entries,), jnp.int32).at[sort_order].set(sorted_rank)
    accepted_booleans = sorting_place < quota_per_class[member_ordinal.reshape(-1)]
    discard_entry = EXPERTS * CAP
    berth_location = jnp.where(accepted_booleans, quota_cell * LARGEST_QUOTA + sorting_place, discard_entry).astype(jnp.int32)
    token_provenance = jnp.full((discard_entry + 1,), token_total, jnp.int32).at[berth_location].set(token_index.reshape(-1))[:discard_entry]
    gate_slots = jnp.zeros((discard_entry + 1,), dispatch_mixing_factors.dtype).at[berth_location].set(dispatch_mixing_factors.reshape(-1))[:discard_entry]
    token_provenance = token_provenance.reshape(N_NODE, N_LOCAL, CAP)
    gate_slots = gate_slots.reshape(N_NODE, N_LOCAL, CAP)
    padded_tokens = jnp.concatenate([input_activation_matrix, jnp.zeros((1, feature), input_activation_matrix.dtype)], axis=0)
    padded_cot = jnp.concatenate([output_adjoint, jnp.zeros((1, feature), output_adjoint.dtype)], axis=0)
    gate_stack = gating_matrix_tensor.reshape(N_NODE, N_LOCAL, D, F)
    up_stack = widening_matrix_tensor.reshape(N_NODE, N_LOCAL, D, F)
    down_stack = shrinking_matrix_tensor.reshape(N_NODE, N_LOCAL, F, D)

    def expert_step(inputs):
        rows_source, gate_vals, weight_gate, weight_up, weight_down = inputs
        row_block = padded_tokens[rows_source]
        upstream = padded_cot[rows_source]
        gate_act, up_act = activations(row_block, weight_gate, weight_up)
        outputs = expert_outputs(gate_act, up_act, weight_down)
        grad_rows, grad_weight = expert_grads(gate_act, up_act, outputs, gate_vals, upstream, weight_gate, weight_up, weight_down)
        weighted = gate_vals.astype(jnp.float32)[:, None] * outputs.astype(jnp.float32)
        return weighted, grad_rows, grad_weight

    def node_step(running, inputs):
        mixed_sum, grad_sum = running
        weighted, grad_rows, grad_weight = lax.map(expert_step, inputs)
        flat_source = inputs[0].reshape(-1)
        part_mixed = jax.ops.segment_sum(weighted.reshape(-1, feature), flat_source, num_segments=token_total + 1)[:token_total]
        part_grad = jax.ops.segment_sum(grad_rows.astype(jnp.float32).reshape(-1, feature), flat_source, num_segments=token_total + 1)[:token_total]
        part_mixed = lax.optimization_barrier(part_mixed.astype(jnp.bfloat16))
        part_grad = lax.optimization_barrier(part_grad.astype(jnp.bfloat16))
        return (mixed_sum + part_mixed.astype(jnp.float32), grad_sum + part_grad.astype(jnp.float32)), grad_weight

    empty_sum = jnp.zeros((token_total, feature), jnp.float32)
    (mixed_sum, grad_sum), weight_slots = lax.scan(node_step, (empty_sum, empty_sum), (token_provenance, gate_slots, gate_stack, up_stack, down_stack))
    linear_coefficients = weight_slots.reshape(-1)
    guarded_location = jnp.where(accepted_booleans, berth_location, 0).astype(jnp.int32)
    coefficient_derivative = jnp.where(accepted_booleans, linear_coefficients[guarded_location], jnp.zeros((), linear_coefficients.dtype))
    coefficient_derivative = coefficient_derivative.astype(jnp.bfloat16).reshape(token_total, TOP)
    return mixed_sum.astype(jnp.bfloat16), grad_sum.astype(jnp.bfloat16), coefficient_derivative
```

```python
import functools
import math
from types import SimpleNamespace

import jax
import jax.numpy as jnp
from jax import lax
from jax.experimental import pallas as pl
from jax.experimental.pallas import tpu as pltpu
from jax.sharding import PartitionSpec as P

MESH = pl.DeviceIdType.MESH
BF = jnp.bfloat16
F32 = jnp.float32


def config(mesh, tok, kg, top, feature, hidden, most=12, quota=48):
    c = SimpleNamespace()
    c.NN, c.NL = mesh.shape["node"], mesh.shape["local"]
    c.NK, c.NX = (2, 8) if c.NN == 64 else (1, 4)
    c.NZ = c.NN // (c.NK * c.NX)
    c.NQ = c.NZ * c.NK
    c.PC = c.NX // 2
    c.D2 = c.NX // 2
    c.NH = c.NX - 1
    c.TOK, c.KG, c.TOP, c.D, c.F = tok, kg, top, feature, hidden
    c.J, c.Q = most, quota
    c.NC = 2
    c.W = feature // c.NC
    c.NS = 2 * c.NC
    c.BL = c.PC * c.J
    c.I = 2 * c.NQ * c.BL
    c.R = c.NL * c.Q
    c.H = tok // 2
    return c


def ring_steps(c):
    right, left = [], []
    for d in range(1, c.D2):
        right += [(d, 0), (d, 1)]
        left += [(d, 1), (d, 0)]
    return right + [(c.D2, 0)], left + [(c.D2, 1)]


def slot_of(c, d, side):
    if d == 0:
        return 0
    return 2 * d - 1 if (side == 0 or d == c.D2) else 2 * d


def plan(c):
    NS, NC, NH = c.NS, c.NC, c.NH
    tx, tz, ty, lat = 1.4, 4.5, 9.0, 1.5
    tasks, links = {}, {}

    def add(key, pri, cost, deps, sends=()):
        tasks[key] = (pri, cost, deps, sends)

    add(("meta1",), -9, 1.5, [], [(("M1",), "x", 0.2)])
    add(("meta2",), -8, 0.5, [("M1",)], [(("M2",), "z", 0.2)])
    add(("pick",), -7, 1.5, [("M1",)])
    add(("rank",), -6, 2.0, [("M2",)])
    for s in range(NS):
        for h in range(NH):
            deps = [("AG", s, h - 2)] if h >= 2 else ([("ag", s - 1, NH - 3)] if s else [])
            add(("ag", s, h), s * 10 - 100, 0.1, deps, [(("AG", s, h), "x", tx)])
        for ch in range(2):
            need = 3 if ch == 0 and c.D2 > 2 else NH - 1
            deps = [("pick",)] + [("AG", s, g) for g in range(need + 1)]
            add(("z", s, ch), s * 10 + ch, 0.8, deps, [(("Z", s, ch), "z", tz)])
        add(("y", s), s * 10 + 3, 0.9, [("rank",), ("Z", s, 0), ("Z", s, 1)], [(("Y", s), "y", ty)])
    for s in range(NS):
        deps = [("Y", s)] + ([("e", s - 1)] if s else [])
        sends = []
        if s == NC - 1:
            sends = [(("B", u), "y", ty) for u in range(NC)]
        if s == NS - 1:
            sends = [(("B", u), "y", ty) for u in range(NC, NS)]
        add(("e", s), s * 10 + 4, 2.0, deps, sends)
        for ch in (1, 0):
            add(("m", s, ch), s * 10 + 5 - ch, 0.8, [("B", s)], [(("RZ", s, ch), "z", tz)])
            add(("p", s, ch), s * 10 + 7 - ch, 0.8, [("RZ", s, ch)])
        for h in range(NH):
            deps = [("p", s, 1)] + ([("p", s, 0)] if h > (2 if c.D2 > 2 else 0) else [])
            deps += [("RS", s, h - 2)] if h >= 2 else []
            add(("rs", s, h), s * 10 - 90, 0.15, deps, [(("RS", s, h), "x", tx)])
        add(("fin", s), s * 10 + 8, 0.3, [("p", s, 0), ("RS", s, NH - 1), ("RS", s, NH - 2)])
    add(("c1",), 45, 1.0, [("m", u, 0) for u in range(NC)] + [("y", u) for u in range(NC, NS)], [(("C1",), "z", 0.2)])
    add(("c2",), 46, 0.2, [("C1",)], [(("C2",), "x", 0.2)])
    add(("c3",), 47, 0.5, [("C2",)])

    done, now, order = {}, 0.0, []
    left = dict(tasks)
    while left:
        best = None
        for key, (pri, cost, deps, sends) in left.items():
            if any(d not in done for d in deps):
                continue
            at = max([done[d] for d in deps], default=0.0)
            rank = (max(at, now), pri, key)
            if best is None or rank < best[0]:
                best = (rank, key)
        key = best[1]
        pri, cost, deps, sends = left.pop(key)
        now = best[0][0] + cost
        done[key] = now
        for event, link, length in sends:
            start = max(now, links.get(link, 0.0))
            links[link] = start + length
            done[event] = start + length + lat
        order.append(key)
    return order, now


def iota(shape, dim):
    return lax.broadcasted_iota(jnp.int32, shape, dim)


def idiv(v, d):
    if d & (d - 1) == 0:
        return lax.shift_right_logical(v, jnp.int32(d.bit_length() - 1)) if d > 1 else v
    return ((v.astype(F32) + 0.5) * (1.0 / d)).astype(jnp.int32)


def imod(v, d):
    if d & (d - 1) == 0:
        return v & (d - 1)
    return v - idiv(v, d) * d


def onehot(mask):
    return jnp.where(mask, 1.0, 0.0).astype(BF)


def mm(a, b):
    return lax.dot_general(a, b, (((1,), (0,)), ((), ())), preferred_element_type=F32)


def mm_nt(a, b):
    return lax.dot_general(a, b, (((1,), (1,)), ((), ())), preferred_element_type=F32)


def kernel(c, order, x_ref, dy_ref, fac_ref, perm_ref, cho_ref, quota_ref, wg_hbm, wu_hbm, wd_hbm,
           mixed_ref, igrad_ref, coef_ref,
           wg, wu, wd, xg, zs, zr, ys, yr, bs, br, rzs, rzr, part, rss, rsr,
           pick, pickt, sel, selt, selg, ag, au, bk, meta, m1, m2s, m2, cm, c1r, c2s, c2r, acat, pmask,
           w_sem, s_small, r_small, ag_s, ag_r, z_s, z_r, y_s, y_r, b_s, b_r, rz_s, rz_r, rs_s, rs_r):
    NX, NQ, NL, PC, J, Q, TOK, NS, NC, W = c.NX, c.NQ, c.NL, c.PC, c.J, c.Q, c.TOK, c.NS, c.NC, c.W
    NG, I, R, BL = c.NN, c.I, c.R, c.BL
    LANES = 128
    node, y = lax.axis_index("node"), lax.axis_index("local")
    k, xx, zz = lax.rem(node, c.NK), lax.rem(lax.div(node, c.NK), NX), lax.div(node, c.NK * NX)
    b_me = zz * c.NK + k

    def x_peer(o):
        return (zz * NX + lax.rem(xx + (o + NX), NX)) * c.NK + k

    def q_peer(i):
        q = lax.rem(b_me + i, NQ)
        return q, (lax.div(q, c.NK) * NX + xx) * c.NK + lax.rem(q, c.NK)

    def y_peer(i):
        return lax.rem(y + i, NL)

    def copy(src, dst, send, recv, to_node, to_local):
        return pltpu.make_async_remote_copy(src_ref=src, dst_ref=dst, send_sem=send, recv_sem=recv,
                                            device_id=(to_node, to_local), device_id_type=MESH)

    def await_recv(like, sem):
        copy(like, like, sem, sem, node, y).wait_recv()

    def await_send(like, sem):
        copy(like, like, sem, sem, node, y).wait_send()

    barrier = pltpu.get_barrier_semaphore()
    for o in range(1, NX):
        pl.semaphore_signal(barrier, inc=1, device_id=(x_peer(o), y), device_id_type=MESH)
    for i in range(1, NQ):
        pl.semaphore_signal(barrier, inc=1, device_id=(q_peer(i)[1], y), device_id_type=MESH)
    for i in range(1, NL):
        pl.semaphore_signal(barrier, inc=1, device_id=(node, y_peer(i)), device_id_type=MESH)

    weights = [pltpu.make_async_copy(h.at[0], v, w_sem.at[n])
               for n, (h, v) in enumerate(((wg_hbm, wg), (wu_hbm, wu), (wd_hbm, wd)))]
    for w in weights:
        w.start()
    for s in range(NS):
        src = x_ref if s < NC else dy_ref
        xg[s, 0] = src[:, (s % NC) * W:(s % NC + 1) * W]
    pl.semaphore_wait(barrier, (NX - 1) + (NQ - 1) + (NL - 1))

    rights, lefts = ring_steps(c)

    def offset_of(p):
        d = lax.shift_right_logical(p + 1, jnp.int32(1))
        return jnp.where((p & 1) == 1, -d, d)

    def static_offset(p):
        d = (p + 1) // 2
        return -d if p % 2 else d

    def do_ag(s, h):
        for side, steps in ((0, rights), (1, lefts)):
            if h >= 2 and (s, h - 2) not in waited:
                d0, h0 = steps[h - 2]
                await_recv(xg.at[s, slot_of(c, d0, side), pl.ds(h0 * c.H, c.H)], ag_r.at[s, side, h - 2])
            d, half = steps[h]
            rows = pl.ds(half * c.H, c.H)
            copy(xg.at[s, slot_of(c, d - 1, side), rows], xg.at[s, slot_of(c, d, side), rows],
                 ag_s.at[s], ag_r.at[s, side, h], x_peer(1 if side == 0 else -1), y).start()

    ag_seen = {s: 0 for s in range(NS)}

    def ag_upto(s, h):
        for g in range(ag_seen[s], h + 1):
            if g + 2 >= c.NH or (("ag", s, g + 2) not in issued):
                for side, steps in ((0, rights), (1, lefts)):
                    d0, h0 = steps[g]
                    await_recv(xg.at[s, slot_of(c, d0, side), pl.ds(h0 * c.H, c.H)], ag_r.at[s, side, g])
                waited.add((s, g))
        ag_seen[s] = max(ag_seen[s], h + 1)

    issued, waited = set(), set()

    def do_meta1():
        perm, cho = perm_ref[...], cho_ref[...]
        fac = fac_ref[...].astype(F32)
        lane = iota((TOK, LANES), 1)
        code = iota((TOK, c.KG * NL), 1)
        table = jnp.zeros((TOK, c.KG * NL), F32)
        for n in range(c.TOP):
            table += jnp.where(cho[:, n:n + 1] == code, fac[:, n:n + 1], 0.0)
        table = table.astype(BF)
        groups = iota((TOK, NG), 1)
        named = []
        for s in range(c.KG):
            g = perm[:, s:s + 1]
            gx = imod(idiv(g, c.NK), NX)
            gq = idiv(g, c.NK * NX) * c.NK + imod(g, c.NK)
            named.append(jnp.where(gx * NQ + gq == groups, 1.0, 0.0))
        total = sum(named[1:], named[0]).astype(BF)
        lower = onehot(iota((TOK, TOK), 1) < iota((TOK, TOK), 0))
        place = mm(lower, total)
        mark = (iota((TOK, LANES), 0) + 1).astype(F32)
        lane_j = idiv(lane, NL)
        out = jnp.zeros((NG, LANES), F32)
        eye = onehot(iota((NG, NG), 0) == iota((NG, NG), 1))
        for s in range(c.KG):
            p = jnp.sum(named[s] * place, axis=1, keepdims=True).astype(jnp.int32)
            spread = onehot((iota((c.KG * NL, LANES), 0) == s * NL + imod(iota((c.KG * NL, LANES), 1), NL)))
            mine = (lane_j == p) & (lane < J * NL)
            rhs = jnp.where(mine, mm(table, spread), 0.0)
            rhs += jnp.where(lane - J * NL == p, mark, 0.0)
            a = named[s].astype(BF)
            out += mm(mm_nt(eye, a).astype(BF), rhs.astype(BF))
            acat[s] = a
            pmask[s] = onehot(mine)
        meta[...] = out.reshape(NX, NQ, LANES)
        m1[0] = meta[xx]
        for p in range(1, NX):
            to = lax.rem(xx + (NX - static_offset(p)), NX)
            copy(meta.at[to], m1.at[p], s_small.at[0], r_small.at[0], (zz * NX + to) * c.NK + k, y).start()

    def do_meta2():
        await_recv(m1.at[pl.ds(0, NX - 1)], r_small.at[0])
        flat = m1[...].reshape(NX * NQ, LANES).astype(BF)
        n = NX * NQ
        row, col = iota((n, n), 0), iota((n, n), 1)
        turn = onehot((imod(row, NX) == idiv(col, NQ)) & (idiv(row, NX) == imod(col, NQ)))
        m2s[...] = mm(turn, flat).reshape(NQ, NX, LANES)
        m2[b_me] = m2s[b_me]
        for i in range(1, NQ):
            q, to = q_peer(i)
            copy(m2s.at[q], m2.at[b_me], s_small.at[1], r_small.at[1], to, y).start()

    def do_pick():
        flat = m1[...].reshape(NX * NQ, LANES).astype(BF)
        C = NQ * BL
        row = iota((C, NX * NQ), 0)
        rq, rp = idiv(row, BL), idiv(imod(row, BL), J)
        lane, lrow = iota((C, LANES), 1), iota((C, LANES), 0)
        rcol = iota((C, 1), 0)
        ccol = iota((1, C), 1)
        for ch in range(2):
            take = onehot((rp + ch * PC) * NQ + rq == iota((C, NX * NQ), 1))
            got = jnp.where(lane == J * NL + imod(lrow, J), mm(take, flat), 0.0)
            down = jnp.sum(got, axis=1, keepdims=True).astype(jnp.int32)
            across = mm_nt(jnp.ones((8, LANES), BF), got.astype(BF))[0:1].astype(jnp.int32)
            down = jnp.where(down > 0, down + TOK * idiv(imod(rcol, BL), J), 0)
            across = jnp.where(across > 0, across + TOK * idiv(imod(ccol, BL), J), 0)
            pick[ch] = onehot(down == iota((C, PC * TOK), 1) + 1)
            pickt[ch] = onehot(across == iota((PC * TOK, C), 0) + 1)

    def slot_rows(v):
        half = NQ * BL
        ch = idiv(v, half)
        rest = v - ch * half
        return idiv(rest, BL) * NX + ch * PC + idiv(imod(rest, BL), J)

    def do_rank():
        await_recv(m2.at[pl.ds(0, NQ - 1)], r_small.at[1])
        n = NQ * NX
        mt = m2[...].reshape(n, LANES)
        lane = iota((n, LANES), 1)
        el = (mt != 0.0) & (lane < J * NL)
        elb = onehot(el)
        l0, l1 = iota((LANES, LANES), 0), iota((LANES, LANES), 1)
        same = (imod(l0, NL) == imod(l1, NL)) & (l0 < J * NL)
        inside = mm(elb, onehot(same & (idiv(l0, NL) < idiv(l1, NL))))
        rows = mm(elb, onehot(same)).astype(BF)

        def number(r):
            b, p = idiv(r, NX), imod(r, NX)
            return (idiv(b, c.NK) * NX + ((xx + offset_of(p) + NX) & (NX - 1))) * c.NK + imod(b, c.NK)

        before = onehot(number(iota((n, n), 1)) < number(iota((n, n), 0)))
        rank = inside + mm(before, rows)
        ql = jnp.broadcast_to(quota_ref[...].astype(F32), (8, NL)).astype(BF)
        ql = mm(ql, onehot(iota((NL, LANES), 0) == imod(iota((NL, LANES), 1), NL)))[0:1]
        keep = el & (rank < ql)
        rk = jnp.where(keep, rank + 1.0, 0.0).astype(BF)
        gk = jnp.where(keep, mt, 0.0).astype(BF)
        eye = onehot(l0 == l1)
        spread = onehot(iota((n, I), 0) == slot_rows(iota((n, I), 1)))
        mine = (idiv(iota((LANES, I), 0), NL) == imod(iota((LANES, I), 1), J)) & (iota((LANES, I), 0) < J * NL)
        fold = onehot((iota((max(NL, 8), LANES), 0) == imod(iota((max(NL, 8), LANES), 1), NL))
                      & (iota((max(NL, 8), LANES), 1) < J * NL))
        flat = jnp.where(mine, mm(mm_nt(eye, rk).astype(BF), spread), 0.0).astype(BF)
        flat = mm(fold, flat)
        for e in range(NL):
            sel[e] = onehot(flat[e:e + 1] == (iota((Q, I), 0) + 1).astype(F32))
        spread = onehot(slot_rows(iota((I, n), 0)) == iota((I, n), 1))
        mine = (idiv(iota((I, LANES), 1), NL) == imod(iota((I, LANES), 0), J)) & (iota((I, LANES), 1) < J * NL)
        widen = onehot((imod(iota((LANES, R), 0), NL) == idiv(iota((LANES, R), 1), Q)) & (iota((LANES, R), 0) < J * NL))
        flat = mm(jnp.where(mine, mm(spread, rk), 0.0).astype(BF), widen)
        gates = mm(jnp.where(mine, mm(spread, gk), 0.0).astype(BF), widen)
        hit = flat == (imod(iota((I, R), 1), Q) + 1).astype(F32)
        selt[...] = onehot(hit)
        selg[...] = jnp.where(hit, gates, 0.0).astype(BF)

    def do_z(s, ch):
        ag_upto(s, 3 if ch == 0 and c.D2 > 2 else c.NH - 1)
        rows = xg[s, ch * PC:(ch + 1) * PC].reshape(PC * TOK, W)
        zs[s, ch] = mm(pick[ch], rows).astype(BF).reshape(NQ, BL, W)
        for i in range(1, NQ):
            q, to = q_peer(i)
            copy(zs.at[s, ch, q], zr.at[s, ch, b_me], z_s.at[s, ch], z_r.at[s, ch], to, y).start()
        zr[s, ch, b_me] = zs[s, ch, b_me]

    def do_y(s):
        for ch in range(2):
            await_recv(zr.at[s, ch, pl.ds(0, NQ - 1)], z_r.at[s, ch])
        ys[s] = mm(sel[...].reshape(R, I), zr[s].reshape(I, W)).astype(BF).reshape(NL, Q, W)
        for i in range(1, NL):
            to = y_peer(i)
            copy(ys.at[s, to], yr.at[s, y], y_s.at[s], y_r.at[s], node, to).start()
        yr[s, y] = ys[s, y]

    def give_back(s, value):
        bs[s] = value.astype(BF).reshape(NL, Q, W)
        for i in range(1, NL):
            to = y_peer(i)
            copy(bs.at[s, to], br.at[s, y], b_s.at[s], b_r.at[s], node, to).start()
        br[s, y] = bs[s, y]

    def do_e(s):
        await_recv(yr.at[s, pl.ds(0, NL - 1)], y_r.at[s])
        rows = yr[s].reshape(R, W)
        u = s % NC
        cols = slice(u * W, (u + 1) * W)
        if s == 0:
            for w in weights:
                w.wait()
        if s < NC:
            a_g, a_u = mm(rows, wg[cols]), mm(rows, wu[cols])
            if u:
                a_g, a_u = a_g + ag[...], a_u + au[...]
            ag[...], au[...] = a_g, a_u
            if s == NC - 1:
                hid = (a_g * jax.nn.sigmoid(a_g) * a_u).astype(BF)
                for v in range(NC):
                    give_back(v, mm(hid, wd[:, v * W:(v + 1) * W]))
        else:
            back = mm_nt(rows, wd[:, cols])
            if u:
                back = back + bk[...]
            bk[...] = back
            if s == NS - 1:
                a_g, a_u = ag[...], au[...]
                sig = jax.nn.sigmoid(a_g)
                g_g = (back * a_u * sig * (1.0 + a_g * (1.0 - sig))).astype(BF)
                g_u = (back * a_g * sig).astype(BF)
                for v in range(NC):
                    rng = slice(v * W, (v + 1) * W)
                    give_back(NC + v, mm_nt(g_g, wg[rng]) + mm_nt(g_u, wu[rng]))

    b_seen = set()

    def do_m(s, ch):
        if s not in b_seen:
            b_seen.add(s)
            await_recv(br.at[s, pl.ds(0, NL - 1)], b_r.at[s])
        half = I // 2
        rzs[s, ch] = mm(selg[ch * half:(ch + 1) * half], br[s].reshape(R, W)).astype(BF).reshape(NQ, BL, W)
        for i in range(1, NQ):
            q, to = q_peer(i)
            copy(rzs.at[s, ch, q], rzr.at[s, ch, b_me], rz_s.at[s, ch], rz_r.at[s, ch], to, y).start()
        rzr[s, ch, b_me] = rzs[s, ch, b_me]

    def do_p(s, ch):
        await_recv(rzr.at[s, ch, pl.ds(0, NQ - 1)], rz_r.at[s, ch])
        part[s, ch * PC:(ch + 1) * PC] = mm(pickt[ch], rzr[s, ch].reshape(NQ * BL, W)).reshape(PC, TOK, W)

    def do_rs(s, h):
        for side, steps in ((0, rights), (1, lefts)):
            d, half = steps[c.NH - 1 - h]
            value = part[s, slot_of(c, d, side), half * c.H:(half + 1) * c.H]
            if h >= 2:
                await_recv(rsr.at[s, side, h - 2], rs_r.at[s, side, h - 2])
                value = value + rsr[s, side, h - 2].astype(F32)
            rss[s, side, h] = value.astype(BF)
            copy(rss.at[s, side, h], rsr.at[s, side, h], rs_s.at[s, side], rs_r.at[s, side, h],
                 x_peer(-1 if side == 0 else 1), y).start()

    def do_fin(s):
        out = mixed_ref if s < NC else igrad_ref
        cols = slice((s % NC) * W, (s % NC + 1) * W)
        values = [part[s, 0, v * c.H:(v + 1) * c.H] for v in range(2)]
        for side, steps in ((0, rights), (1, lefts)):
            for h in (c.NH - 2, c.NH - 1):
                await_recv(rsr.at[s, side, h], rs_r.at[s, side, h])
                half = steps[c.NH - 1 - h][1]
                values[half] = values[half] + rsr[s, side, h].astype(F32)
        for v in range(2):
            out[v * c.H:(v + 1) * c.H, cols] = values[v].astype(BF)

    def do_c1():
        cd = jnp.zeros((R, 1), F32)
        for u in range(NC):
            cd += jnp.sum(ys[NC + u].reshape(R, W).astype(F32) * br[u].reshape(R, W).astype(F32), axis=1, keepdims=True)
        spread = jnp.where(idiv(iota((R, LANES), 0), Q) == imod(iota((R, LANES), 1), NL), cd, 0.0).astype(BF)
        got = mm(selt[...], spread)
        mine = (idiv(iota((I, LANES), 1), NL) == imod(iota((I, LANES), 0), J)) & (iota((I, LANES), 1) < J * NL)
        got = jnp.where(mine, got, 0.0).astype(BF)
        n = NQ * NX
        fold = onehot(iota((n, I), 0) == slot_rows(iota((n, I), 1)))
        cm[...] = mm(fold, got).reshape(NQ, NX, LANES)
        c1r[b_me] = cm[b_me]
        for i in range(1, NQ):
            q, to = q_peer(i)
            copy(cm.at[q], c1r.at[b_me], s_small.at[2], r_small.at[2], to, y).start()

    def do_c2():
        await_recv(c1r.at[pl.ds(0, NQ - 1)], r_small.at[2])
        n = NX * NQ
        row, col = iota((n, n), 0), iota((n, n), 1)
        turn = onehot((imod(row, NQ) == idiv(col, NX)) & (idiv(row, NQ) == imod(col, NX)))
        c2s[...] = mm(turn, c1r[...].reshape(n, LANES).astype(BF)).reshape(NX, NQ, LANES)
        c2r[xx] = c2s[0]
        for p in range(1, NX):
            to = lax.rem(xx + (static_offset(p) + NX), NX)
            copy(c2s.at[p], c2r.at[xx], s_small.at[3], r_small.at[3], (zz * NX + to) * c.NK + k, y).start()

    def do_c3():
        await_recv(c2r.at[pl.ds(0, NX - 1)], r_small.at[3])
        rows = c2r[...].reshape(NX * NQ, LANES).astype(BF)
        codes = c.KG * NL
        tab = jnp.zeros((TOK, codes), F32)
        for s in range(c.KG):
            mine = mm(acat[s], rows) * pmask[s].astype(F32)
            spread = onehot((iota((codes, LANES), 0) == s * NL + imod(iota((codes, LANES), 1), NL)))
            tab += mm_nt(mine.astype(BF), spread)
        cho = cho_ref[...]
        code, entry = iota((TOK, codes), 1), iota((TOK, c.TOP), 1)
        out = jnp.zeros((TOK, c.TOP), F32)
        for n in range(c.TOP):
            value = jnp.sum(jnp.where(cho[:, n:n + 1] == code, tab, 0.0), axis=1, keepdims=True)
            out += jnp.where(entry == n, value, 0.0)
        coef_ref[...] = out.astype(BF)

    steps = {"ag": do_ag, "z": do_z, "y": do_y, "e": do_e, "m": do_m, "p": do_p, "rs": do_rs, "fin": do_fin,
             "meta1": do_meta1, "meta2": do_meta2, "pick": do_pick, "rank": do_rank,
             "c1": do_c1, "c2": do_c2, "c3": do_c3}
    for key in order:
        steps[key[0]](*key[1:])
        issued.add(key)

    for n, ref in enumerate((m1.at[pl.ds(0, NX - 1)], m2.at[pl.ds(0, NQ - 1)], c1r.at[pl.ds(0, NQ - 1)],
                             c2r.at[pl.ds(0, NX - 1)])):
        await_send(ref, s_small.at[n])
    for s in range(NS):
        await_send(xg.at[s, pl.ds(0, NX - 1)], ag_s.at[s])
        for ref, sem in ((zs, z_s), (rzs, rz_s)):
            for ch in range(2):
                await_send(ref.at[s, ch, pl.ds(0, NQ - 1)], sem.at[s, ch])
        await_send(ys.at[s, pl.ds(0, NL - 1)], y_s.at[s])
        await_send(bs.at[s, pl.ds(0, NL - 1)], b_s.at[s])
        for side in range(2):
            await_send(rss.at[s, side], rs_s.at[s, side])


def per_device(c, x, dy, fac, perm, cho, quota, wg, wu, wd):
    NX, NQ, NL, PC, J, Q, TOK, NS, W = c.NX, c.NQ, c.NL, c.PC, c.J, c.Q, c.TOK, c.NS, c.W
    order, _ = plan(c)
    dma = pltpu.SemaphoreType.DMA
    V = pltpu.VMEM
    C = NQ * c.BL
    scratch = [
        V((c.D, c.F), BF), V((c.D, c.F), BF), V((c.F, c.D), BF),
        V((NS, NX, TOK, W), BF),
        V((NS, 2, NQ, c.BL, W), BF), V((NS, 2, NQ, c.BL, W), BF),
        V((NS, NL, Q, W), BF), V((NS, NL, Q, W), BF),
        V((NS, NL, Q, W), BF), V((NS, NL, Q, W), BF),
        V((NS, 2, NQ, c.BL, W), BF), V((NS, 2, NQ, c.BL, W), BF),
        V((NS, NX, TOK, W), F32),
        V((NS, 2, c.NH, c.H, W), BF), V((NS, 2, c.NH, c.H, W), BF),
        V((2, C, PC * TOK), BF), V((2, PC * TOK, C), BF),
        V((NL, Q, c.I), BF), V((c.I, c.R), BF), V((c.I, c.R), BF),
        V((c.R, c.F), F32), V((c.R, c.F), F32), V((c.R, c.F), F32),
        V((NX, NQ, 128), F32), V((NX, NQ, 128), F32), V((NQ, NX, 128), F32), V((NQ, NX, 128), F32),
        V((NQ, NX, 128), F32), V((NQ, NX, 128), F32), V((NX, NQ, 128), F32), V((NX, NQ, 128), F32),
        V((c.KG, TOK, c.NN), BF), V((c.KG, TOK, 128), BF),
        dma((3,)), dma((4,)), dma((4,)),
        dma((NS,)), dma((NS, 2, c.NH)), dma((NS, 2)), dma((NS, 2)), dma((NS,)), dma((NS,)),
        dma((NS,)), dma((NS,)), dma((NS, 2)), dma((NS, 2)), dma((NS, 2)), dma((NS, 2, c.NH)),
    ]
    vm = pl.BlockSpec(memory_space=pltpu.VMEM)
    hbm = pl.BlockSpec(memory_space=pl.ANY)
    flops = 2 * c.R * c.D * c.F * 6
    return pl.pallas_call(
        functools.partial(kernel, c, order),
        out_shape=(jax.ShapeDtypeStruct((TOK, c.D), BF), jax.ShapeDtypeStruct((TOK, c.D), BF),
                   jax.ShapeDtypeStruct((TOK, c.TOP), BF)),
        in_specs=[vm] * 6 + [hbm] * 3,
        out_specs=(vm, vm, vm),
        scratch_shapes=scratch,
        compiler_params=pltpu.CompilerParams(collective_id=0, has_side_effects=True, vmem_limit_bytes=60 * 2**20),
        cost_estimate=pl.CostEstimate(flops=flops, bytes_accessed=4 * 2**20, transcendentals=c.R * c.F),
        name="expert_layer",
    )(x, dy, fac, perm, cho, quota.reshape(1, NL), wg, wu, wd)


def solution(mesh, **over):
    def step(x, dy, fac, perm, cho, quota, wg, wu, wd):
        c = config(mesh, x.shape[0], perm.shape[1], cho.shape[1], x.shape[1], wg.shape[2], **over)
        return per_device(c, x, dy, fac, perm, cho, quota, wg, wu, wd)

    rows = P(("node", "local"), None)
    cube = P(("node", "local"), None, None)
    return jax.shard_map(
        step,
        mesh=mesh,
        in_specs=(rows, rows, rows, rows, rows, P("node"), cube, cube, cube),
        out_specs=(rows, rows, rows),
        check_vma=False,
    )
```

```python
import functools
import math
from types import SimpleNamespace

import jax
import jax.numpy as jnp
from jax import lax
from jax.experimental import pallas as pl
from jax.experimental.pallas import tpu as pltpu
from jax.sharding import PartitionSpec as P

MESH = pl.DeviceIdType.MESH
BF = jnp.bfloat16
F32 = jnp.float32


def config(mesh, tok, kg, top, feature, hidden, most=12, quota=48):
    c = SimpleNamespace()
    c.NN, c.NL = mesh.shape["node"], mesh.shape["local"]
    c.NX = 8 if c.NN == 64 else 4
    c.NQ = c.NN // c.NX
    c.PC = c.NX // 2
    c.D2 = c.NX // 2
    c.NH = c.NX - 1
    c.TOK, c.KG, c.TOP, c.D, c.F = tok, kg, top, feature, hidden
    c.J, c.Q = most, quota
    c.NC = 2
    c.W = feature // c.NC
    c.NS = 2 * c.NC
    c.BL = c.PC * c.J
    c.I = 2 * c.NQ * c.BL
    c.R = c.NL * c.Q
    c.H = tok // 2
    return c


def ring_steps(c):
    right, left = [], []
    for d in range(1, c.D2):
        right += [(d, 0), (d, 1)]
        left += [(d, 1), (d, 0)]
    return right + [(c.D2, 0)], left + [(c.D2, 1)]


def slot_of(c, d, side):
    if d == 0:
        return 0
    return 2 * d - 1 if (side == 0 or d == c.D2) else 2 * d


def plan(c):
    NS, NC, NH = c.NS, c.NC, c.NH
    tx, tz, ty, lat = 1.4, 4.5, 9.0, 1.5
    tasks, links = {}, {}

    def add(key, pri, cost, deps, sends=()):
        tasks[key] = (pri, cost, deps, sends)

    add(("meta1",), -9, 1.5, [], [(("M1",), "x", 0.2)])
    add(("meta2",), -8, 0.5, [("M1",)], [(("M2",), "z", 0.2)])
    add(("pick",), -7, 1.5, [("M1",)])
    add(("rank",), -6, 2.0, [("M2",)])
    for s in range(NS):
        for h in range(NH):
            deps = [("AG", s, h - 2)] if h >= 2 else ([("ag", s - 1, NH - 3)] if s else [])
            add(("ag", s, h), s * 10 - 100, 0.1, deps, [(("AG", s, h), "x", tx)])
        for ch in range(2):
            need = 3 if ch == 0 and c.D2 > 2 else NH - 1
            deps = [("pick",)] + [("AG", s, g) for g in range(need + 1)]
            add(("z", s, ch), s * 10 + ch, 0.8, deps, [(("Z", s, ch), "z", tz)])
        add(("y", s), s * 10 + 3, 0.9, [("rank",), ("Z", s, 0), ("Z", s, 1)], [(("Y", s), "y", ty)])
    for s in range(NS):
        deps = [("Y", s)] + ([("e", s - 1)] if s else [])
        sends = []
        if s == NC - 1:
            sends = [(("B", u), "y", ty) for u in range(NC)]
        if s == NS - 1:
            sends = [(("B", u), "y", ty) for u in range(NC, NS)]
        add(("e", s), s * 10 + 4, 2.0, deps, sends)
        for ch in (1, 0):
            add(("m", s, ch), s * 10 + 5 - ch, 0.8, [("B", s)], [(("RZ", s, ch), "z", tz)])
            add(("p", s, ch), s * 10 + 7 - ch, 0.8, [("RZ", s, ch)])
        for h in range(NH):
            deps = [("p", s, 1)] + ([("p", s, 0)] if h > (2 if c.D2 > 2 else 0) else [])
            deps += [("RS", s, h - 2)] if h >= 2 else []
            add(("rs", s, h), s * 10 - 90, 0.15, deps, [(("RS", s, h), "x", tx)])
        add(("fin", s), s * 10 + 8, 0.3, [("p", s, 0), ("RS", s, NH - 1), ("RS", s, NH - 2)])
    add(("c1",), 45, 1.0, [("m", u, 0) for u in range(NC)] + [("y", u) for u in range(NC, NS)], [(("C1",), "z", 0.2)])
    add(("c2",), 46, 0.2, [("C1",)], [(("C2",), "x", 0.2)])
    add(("c3",), 47, 0.5, [("C2",)])

    done, now, order = {}, 0.0, []
    left = dict(tasks)
    while left:
        best = None
        for key, (pri, cost, deps, sends) in left.items():
            if any(d not in done for d in deps):
                continue
            at = max([done[d] for d in deps], default=0.0)
            rank = (max(at, now), pri, key)
            if best is None or rank < best[0]:
                best = (rank, key)
        key = best[1]
        pri, cost, deps, sends = left.pop(key)
        now = best[0][0] + cost
        done[key] = now
        for event, link, length in sends:
            start = max(now, links.get(link, 0.0))
            links[link] = start + length
            done[event] = start + length + lat
        order.append(key)
    return order, now


def iota(shape, dim):
    return lax.broadcasted_iota(jnp.int32, shape, dim)


def idiv(v, d):
    if d & (d - 1) == 0:
        return lax.shift_right_logical(v, jnp.int32(d.bit_length() - 1)) if d > 1 else v
    return ((v.astype(F32) + 0.5) * (1.0 / d)).astype(jnp.int32)


def imod(v, d):
    if d & (d - 1) == 0:
        return v & (d - 1)
    return v - idiv(v, d) * d


def onehot(mask):
    return jnp.where(mask, 1.0, 0.0).astype(BF)


def mm(a, b):
    return lax.dot_general(a, b, (((1,), (0,)), ((), ())), preferred_element_type=F32)


def mm_nt(a, b):
    return lax.dot_general(a, b, (((1,), (1,)), ((), ())), preferred_element_type=F32)


def kernel(c, order, x_ref, dy_ref, fac_ref, perm_ref, cho_ref, quota_ref, wg_hbm, wu_hbm, wd_hbm,
           mixed_ref, igrad_ref, coef_ref,
           wg, wu, wd, xg, zs, zr, ys, yr, bs, br, rzs, rzr, part, rss, rsr,
           pick, pickt, sel, selt, selg, ag, au, bk, meta, m1, m2s, m2, cm, c1r, c2s, c2r, acat, pmask,
           w_sem, s_small, r_small, ag_s, ag_r, z_s, z_r, y_s, y_r, b_s, b_r, rz_s, rz_r, rs_s, rs_r):
    NX, NQ, NL, PC, J, Q, TOK, NS, NC, W = c.NX, c.NQ, c.NL, c.PC, c.J, c.Q, c.TOK, c.NS, c.NC, c.W
    NG, I, R, BL = c.NN, c.I, c.R, c.BL
    LANES = 128
    node, y = lax.axis_index("node"), lax.axis_index("local")
    xx, b_me = lax.div(node, NQ), lax.rem(node, NQ)

    def x_peer(o):
        return lax.rem(xx + (o + NX), NX) * NQ + b_me

    def q_peer(i):
        q = lax.rem(b_me + i, NQ)
        return q, xx * NQ + q

    def y_peer(i):
        return lax.rem(y + i, NL)

    def copy(src, dst, send, recv, to_node, to_local):
        return pltpu.make_async_remote_copy(src_ref=src, dst_ref=dst, send_sem=send, recv_sem=recv,
                                            device_id=(to_node, to_local), device_id_type=MESH)

    def await_recv(like, sem):
        copy(like, like, sem, sem, node, y).wait_recv()

    def await_send(like, sem):
        copy(like, like, sem, sem, node, y).wait_send()

    barrier = pltpu.get_barrier_semaphore()
    for o in range(1, NX):
        pl.semaphore_signal(barrier, inc=1, device_id=(x_peer(o), y), device_id_type=MESH)
    for i in range(1, NQ):
        pl.semaphore_signal(barrier, inc=1, device_id=(q_peer(i)[1], y), device_id_type=MESH)
    for i in range(1, NL):
        pl.semaphore_signal(barrier, inc=1, device_id=(node, y_peer(i)), device_id_type=MESH)

    weights = [pltpu.make_async_copy(h.at[0], v, w_sem.at[n])
               for n, (h, v) in enumerate(((wg_hbm, wg), (wu_hbm, wu), (wd_hbm, wd)))]
    for w in weights:
        w.start()
    for s in range(NS):
        src = x_ref if s < NC else dy_ref
        xg[s, 0] = src[:, (s % NC) * W:(s % NC + 1) * W]
    pl.semaphore_wait(barrier, (NX - 1) + (NQ - 1) + (NL - 1))

    rights, lefts = ring_steps(c)

    def offset_of(p):
        d = lax.shift_right_logical(p + 1, jnp.int32(1))
        return jnp.where((p & 1) == 1, -d, d)

    def static_offset(p):
        d = (p + 1) // 2
        return -d if p % 2 else d

    def do_ag(s, h):
        for side, steps in ((0, rights), (1, lefts)):
            if h >= 2 and (s, h - 2) not in waited:
                d0, h0 = steps[h - 2]
                await_recv(xg.at[s, slot_of(c, d0, side), pl.ds(h0 * c.H, c.H)], ag_r.at[s, side, h - 2])
            d, half = steps[h]
            rows = pl.ds(half * c.H, c.H)
            copy(xg.at[s, slot_of(c, d - 1, side), rows], xg.at[s, slot_of(c, d, side), rows],
                 ag_s.at[s], ag_r.at[s, side, h], x_peer(1 if side == 0 else -1), y).start()

    ag_seen = {s: 0 for s in range(NS)}

    def ag_upto(s, h):
        for g in range(ag_seen[s], h + 1):
            if g + 2 >= c.NH or (("ag", s, g + 2) not in issued):
                for side, steps in ((0, rights), (1, lefts)):
                    d0, h0 = steps[g]
                    await_recv(xg.at[s, slot_of(c, d0, side), pl.ds(h0 * c.H, c.H)], ag_r.at[s, side, g])
                waited.add((s, g))
        ag_seen[s] = max(ag_seen[s], h + 1)

    issued, waited = set(), set()

    def do_meta1():
        perm, cho = perm_ref[...], cho_ref[...]
        fac = fac_ref[...].astype(F32)
        lane = iota((TOK, LANES), 1)
        code = iota((TOK, c.KG * NL), 1)
        table = jnp.zeros((TOK, c.KG * NL), F32)
        for n in range(c.TOP):
            table += jnp.where(cho[:, n:n + 1] == code, fac[:, n:n + 1], 0.0)
        table = table.astype(BF)
        groups = iota((TOK, NG), 1)
        named = []
        for s in range(c.KG):
            g = perm[:, s:s + 1]
            named.append(jnp.where(g == groups, 1.0, 0.0))
        total = sum(named[1:], named[0]).astype(BF)
        lower = onehot(iota((TOK, TOK), 1) < iota((TOK, TOK), 0))
        place = mm(lower, total)
        mark = (iota((TOK, LANES), 0) + 1).astype(F32)
        lane_j = idiv(lane, NL)
        out = jnp.zeros((NG, LANES), F32)
        eye = onehot(iota((NG, NG), 0) == iota((NG, NG), 1))
        for s in range(c.KG):
            p = jnp.sum(named[s] * place, axis=1, keepdims=True).astype(jnp.int32)
            spread = onehot((iota((c.KG * NL, LANES), 0) == s * NL + imod(iota((c.KG * NL, LANES), 1), NL)))
            mine = (lane_j == p) & (lane < J * NL)
            rhs = jnp.where(mine, mm(table, spread), 0.0)
            rhs += jnp.where(lane - J * NL == p, mark, 0.0)
            a = named[s].astype(BF)
            out += mm(mm_nt(eye, a).astype(BF), rhs.astype(BF))
            acat[s] = a
            pmask[s] = onehot(mine)
        meta[...] = out.reshape(NX, NQ, LANES)
        m1[0] = meta[xx]
        for p in range(1, NX):
            to = lax.rem(xx + (NX - static_offset(p)), NX)
            copy(meta.at[to], m1.at[p], s_small.at[0], r_small.at[0], to * NQ + b_me, y).start()

    def do_meta2():
        await_recv(m1.at[pl.ds(0, NX - 1)], r_small.at[0])
        flat = m1[...].reshape(NX * NQ, LANES).astype(BF)
        n = NX * NQ
        row, col = iota((n, n), 0), iota((n, n), 1)
        turn = onehot((imod(row, NX) == idiv(col, NQ)) & (idiv(row, NX) == imod(col, NQ)))
        m2s[...] = mm(turn, flat).reshape(NQ, NX, LANES)
        m2[b_me] = m2s[b_me]
        for i in range(1, NQ):
            q, to = q_peer(i)
            copy(m2s.at[q], m2.at[b_me], s_small.at[1], r_small.at[1], to, y).start()

    def do_pick():
        flat = m1[...].reshape(NX * NQ, LANES).astype(BF)
        C = NQ * BL
        row = iota((C, NX * NQ), 0)
        rq, rp = idiv(row, BL), idiv(imod(row, BL), J)
        lane, lrow = iota((C, LANES), 1), iota((C, LANES), 0)
        rcol = iota((C, 1), 0)
        ccol = iota((1, C), 1)
        for ch in range(2):
            take = onehot((rp + ch * PC) * NQ + rq == iota((C, NX * NQ), 1))
            got = jnp.where(lane == J * NL + imod(lrow, J), mm(take, flat), 0.0)
            down = jnp.sum(got, axis=1, keepdims=True).astype(jnp.int32)
            across = mm_nt(jnp.ones((8, LANES), BF), got.astype(BF))[0:1].astype(jnp.int32)
            down = jnp.where(down > 0, down + TOK * idiv(imod(rcol, BL), J), 0)
            across = jnp.where(across > 0, across + TOK * idiv(imod(ccol, BL), J), 0)
            pick[ch] = onehot(down == iota((C, PC * TOK), 1) + 1)
            pickt[ch] = onehot(across == iota((PC * TOK, C), 0) + 1)

    def slot_rows(v):
        half = NQ * BL
        ch = idiv(v, half)
        rest = v - ch * half
        return idiv(rest, BL) * NX + ch * PC + idiv(imod(rest, BL), J)

    def do_rank():
        await_recv(m2.at[pl.ds(0, NQ - 1)], r_small.at[1])
        n = NQ * NX
        mt = m2[...].reshape(n, LANES)
        lane = iota((n, LANES), 1)
        el = (mt != 0.0) & (lane < J * NL)
        elb = onehot(el)
        l0, l1 = iota((LANES, LANES), 0), iota((LANES, LANES), 1)
        same = (imod(l0, NL) == imod(l1, NL)) & (l0 < J * NL)
        inside = mm(elb, onehot(same & (idiv(l0, NL) < idiv(l1, NL))))
        rows = mm(elb, onehot(same)).astype(BF)

        def number(r):
            b, p = idiv(r, NX), imod(r, NX)
            return ((xx + offset_of(p) + NX) & (NX - 1)) * NQ + b

        before = onehot(number(iota((n, n), 1)) < number(iota((n, n), 0)))
        rank = inside + mm(before, rows)
        ql = jnp.broadcast_to(quota_ref[...].astype(F32), (8, NL)).astype(BF)
        ql = mm(ql, onehot(iota((NL, LANES), 0) == imod(iota((NL, LANES), 1), NL)))[0:1]
        keep = el & (rank < ql)
        rk = jnp.where(keep, rank + 1.0, 0.0).astype(BF)
        gk = jnp.where(keep, mt, 0.0).astype(BF)
        eye = onehot(l0 == l1)
        spread = onehot(iota((n, I), 0) == slot_rows(iota((n, I), 1)))
        mine = (idiv(iota((LANES, I), 0), NL) == imod(iota((LANES, I), 1), J)) & (iota((LANES, I), 0) < J * NL)
        fold = onehot((iota((max(NL, 8), LANES), 0) == imod(iota((max(NL, 8), LANES), 1), NL))
                      & (iota((max(NL, 8), LANES), 1) < J * NL))
        flat = jnp.where(mine, mm(mm_nt(eye, rk).astype(BF), spread), 0.0).astype(BF)
        flat = mm(fold, flat)
        for e in range(NL):
            sel[e] = onehot(flat[e:e + 1] == (iota((Q, I), 0) + 1).astype(F32))
        spread = onehot(slot_rows(iota((I, n), 0)) == iota((I, n), 1))
        mine = (idiv(iota((I, LANES), 1), NL) == imod(iota((I, LANES), 0), J)) & (iota((I, LANES), 1) < J * NL)
        widen = onehot((imod(iota((LANES, R), 0), NL) == idiv(iota((LANES, R), 1), Q)) & (iota((LANES, R), 0) < J * NL))
        flat = mm(jnp.where(mine, mm(spread, rk), 0.0).astype(BF), widen)
        gates = mm(jnp.where(mine, mm(spread, gk), 0.0).astype(BF), widen)
        hit = flat == (imod(iota((I, R), 1), Q) + 1).astype(F32)
        selt[...] = onehot(hit)
        selg[...] = jnp.where(hit, gates, 0.0).astype(BF)

    def do_z(s, ch):
        ag_upto(s, 3 if ch == 0 and c.D2 > 2 else c.NH - 1)
        rows = xg[s, ch * PC:(ch + 1) * PC].reshape(PC * TOK, W)
        zs[s, ch] = mm(pick[ch], rows).astype(BF).reshape(NQ, BL, W)
        for i in range(1, NQ):
            q, to = q_peer(i)
            copy(zs.at[s, ch, q], zr.at[s, ch, b_me], z_s.at[s, ch], z_r.at[s, ch], to, y).start()
        zr[s, ch, b_me] = zs[s, ch, b_me]

    def do_y(s):
        for ch in range(2):
            await_recv(zr.at[s, ch, pl.ds(0, NQ - 1)], z_r.at[s, ch])
        ys[s] = mm(sel[...].reshape(R, I), zr[s].reshape(I, W)).astype(BF).reshape(NL, Q, W)
        for i in range(1, NL):
            to = y_peer(i)
            copy(ys.at[s, to], yr.at[s, y], y_s.at[s], y_r.at[s], node, to).start()
        yr[s, y] = ys[s, y]

    def give_back(s, value):
        bs[s] = value.astype(BF).reshape(NL, Q, W)
        for i in range(1, NL):
            to = y_peer(i)
            copy(bs.at[s, to], br.at[s, y], b_s.at[s], b_r.at[s], node, to).start()
        br[s, y] = bs[s, y]

    def do_e(s):
        await_recv(yr.at[s, pl.ds(0, NL - 1)], y_r.at[s])
        rows = yr[s].reshape(R, W)
        u = s % NC
        cols = slice(u * W, (u + 1) * W)
        if s == 0:
            for w in weights:
                w.wait()
        if s < NC:
            a_g, a_u = mm(rows, wg[cols]), mm(rows, wu[cols])
            if u:
                a_g, a_u = a_g + ag[...], a_u + au[...]
            ag[...], au[...] = a_g, a_u
            if s == NC - 1:
                hid = (a_g * jax.nn.sigmoid(a_g) * a_u).astype(BF)
                for v in range(NC):
                    give_back(v, mm(hid, wd[:, v * W:(v + 1) * W]))
        else:
            back = mm_nt(rows, wd[:, cols])
            if u:
                back = back + bk[...]
            bk[...] = back
            if s == NS - 1:
                a_g, a_u = ag[...], au[...]
                sig = jax.nn.sigmoid(a_g)
                g_g = (back * a_u * sig * (1.0 + a_g * (1.0 - sig))).astype(BF)
                g_u = (back * a_g * sig).astype(BF)
                for v in range(NC):
                    rng = slice(v * W, (v + 1) * W)
                    give_back(NC + v, mm_nt(g_g, wg[rng]) + mm_nt(g_u, wu[rng]))

    b_seen = set()

    def do_m(s, ch):
        if s not in b_seen:
            b_seen.add(s)
            await_recv(br.at[s, pl.ds(0, NL - 1)], b_r.at[s])
        half = I // 2
        rzs[s, ch] = mm(selg[ch * half:(ch + 1) * half], br[s].reshape(R, W)).astype(BF).reshape(NQ, BL, W)
        for i in range(1, NQ):
            q, to = q_peer(i)
            copy(rzs.at[s, ch, q], rzr.at[s, ch, b_me], rz_s.at[s, ch], rz_r.at[s, ch], to, y).start()
        rzr[s, ch, b_me] = rzs[s, ch, b_me]

    def do_p(s, ch):
        await_recv(rzr.at[s, ch, pl.ds(0, NQ - 1)], rz_r.at[s, ch])
        part[s, ch * PC:(ch + 1) * PC] = mm(pickt[ch], rzr[s, ch].reshape(NQ * BL, W)).reshape(PC, TOK, W)

    def do_rs(s, h):
        for side, steps in ((0, rights), (1, lefts)):
            d, half = steps[c.NH - 1 - h]
            value = part[s, slot_of(c, d, side), half * c.H:(half + 1) * c.H]
            if h >= 2:
                await_recv(rsr.at[s, side, h - 2], rs_r.at[s, side, h - 2])
                value = value + rsr[s, side, h - 2].astype(F32)
            rss[s, side, h] = value.astype(BF)
            copy(rss.at[s, side, h], rsr.at[s, side, h], rs_s.at[s, side], rs_r.at[s, side, h],
                 x_peer(-1 if side == 0 else 1), y).start()

    def do_fin(s):
        out = mixed_ref if s < NC else igrad_ref
        cols = slice((s % NC) * W, (s % NC + 1) * W)
        values = [part[s, 0, v * c.H:(v + 1) * c.H] for v in range(2)]
        for side, steps in ((0, rights), (1, lefts)):
            for h in (c.NH - 2, c.NH - 1):
                await_recv(rsr.at[s, side, h], rs_r.at[s, side, h])
                half = steps[c.NH - 1 - h][1]
                values[half] = values[half] + rsr[s, side, h].astype(F32)
        for v in range(2):
            out[v * c.H:(v + 1) * c.H, cols] = values[v].astype(BF)

    def do_c1():
        cd = jnp.zeros((R, 1), F32)
        for u in range(NC):
            cd += jnp.sum(ys[NC + u].reshape(R, W).astype(F32) * br[u].reshape(R, W).astype(F32), axis=1, keepdims=True)
        spread = jnp.where(idiv(iota((R, LANES), 0), Q) == imod(iota((R, LANES), 1), NL), cd, 0.0).astype(BF)
        got = mm(selt[...], spread)
        mine = (idiv(iota((I, LANES), 1), NL) == imod(iota((I, LANES), 0), J)) & (iota((I, LANES), 1) < J * NL)
        got = jnp.where(mine, got, 0.0).astype(BF)
        n = NQ * NX
        fold = onehot(iota((n, I), 0) == slot_rows(iota((n, I), 1)))
        cm[...] = mm(fold, got).reshape(NQ, NX, LANES)
        c1r[b_me] = cm[b_me]
        for i in range(1, NQ):
            q, to = q_peer(i)
            copy(cm.at[q], c1r.at[b_me], s_small.at[2], r_small.at[2], to, y).start()

    def do_c2():
        await_recv(c1r.at[pl.ds(0, NQ - 1)], r_small.at[2])
        n = NX * NQ
        row, col = iota((n, n), 0), iota((n, n), 1)
        turn = onehot((imod(row, NQ) == idiv(col, NX)) & (idiv(row, NQ) == imod(col, NX)))
        c2s[...] = mm(turn, c1r[...].reshape(n, LANES).astype(BF)).reshape(NX, NQ, LANES)
        c2r[xx] = c2s[0]
        for p in range(1, NX):
            to = lax.rem(xx + (static_offset(p) + NX), NX)
            copy(c2s.at[p], c2r.at[xx], s_small.at[3], r_small.at[3], to * NQ + b_me, y).start()

    def do_c3():
        await_recv(c2r.at[pl.ds(0, NX - 1)], r_small.at[3])
        rows = c2r[...].reshape(NX * NQ, LANES).astype(BF)
        codes = c.KG * NL
        tab = jnp.zeros((TOK, codes), F32)
        for s in range(c.KG):
            mine = mm(acat[s], rows) * pmask[s].astype(F32)
            spread = onehot((iota((codes, LANES), 0) == s * NL + imod(iota((codes, LANES), 1), NL)))
            tab += mm_nt(mine.astype(BF), spread)
        cho = cho_ref[...]
        code, entry = iota((TOK, codes), 1), iota((TOK, c.TOP), 1)
        out = jnp.zeros((TOK, c.TOP), F32)
        for n in range(c.TOP):
            value = jnp.sum(jnp.where(cho[:, n:n + 1] == code, tab, 0.0), axis=1, keepdims=True)
            out += jnp.where(entry == n, value, 0.0)
        coef_ref[...] = out.astype(BF)

    steps = {"ag": do_ag, "z": do_z, "y": do_y, "e": do_e, "m": do_m, "p": do_p, "rs": do_rs, "fin": do_fin,
             "meta1": do_meta1, "meta2": do_meta2, "pick": do_pick, "rank": do_rank,
             "c1": do_c1, "c2": do_c2, "c3": do_c3}
    for key in order:
        steps[key[0]](*key[1:])
        issued.add(key)

    for n, ref in enumerate((m1.at[pl.ds(0, NX - 1)], m2.at[pl.ds(0, NQ - 1)], c1r.at[pl.ds(0, NQ - 1)],
                             c2r.at[pl.ds(0, NX - 1)])):
        await_send(ref, s_small.at[n])
    for s in range(NS):
        await_send(xg.at[s, pl.ds(0, NX - 1)], ag_s.at[s])
        for ref, sem in ((zs, z_s), (rzs, rz_s)):
            for ch in range(2):
                await_send(ref.at[s, ch, pl.ds(0, NQ - 1)], sem.at[s, ch])
        await_send(ys.at[s, pl.ds(0, NL - 1)], y_s.at[s])
        await_send(bs.at[s, pl.ds(0, NL - 1)], b_s.at[s])
        for side in range(2):
            await_send(rss.at[s, side], rs_s.at[s, side])


def per_device(c, x, dy, fac, perm, cho, quota, wg, wu, wd):
    NX, NQ, NL, PC, J, Q, TOK, NS, W = c.NX, c.NQ, c.NL, c.PC, c.J, c.Q, c.TOK, c.NS, c.W
    order, _ = plan(c)
    dma = pltpu.SemaphoreType.DMA
    V = pltpu.VMEM
    C = NQ * c.BL
    scratch = [
        V((c.D, c.F), BF), V((c.D, c.F), BF), V((c.F, c.D), BF),
        V((NS, NX, TOK, W), BF),
        V((NS, 2, NQ, c.BL, W), BF), V((NS, 2, NQ, c.BL, W), BF),
        V((NS, NL, Q, W), BF), V((NS, NL, Q, W), BF),
        V((NS, NL, Q, W), BF), V((NS, NL, Q, W), BF),
        V((NS, 2, NQ, c.BL, W), BF), V((NS, 2, NQ, c.BL, W), BF),
        V((NS, NX, TOK, W), F32),
        V((NS, 2, c.NH, c.H, W), BF), V((NS, 2, c.NH, c.H, W), BF),
        V((2, C, PC * TOK), BF), V((2, PC * TOK, C), BF),
        V((NL, Q, c.I), BF), V((c.I, c.R), BF), V((c.I, c.R), BF),
        V((c.R, c.F), F32), V((c.R, c.F), F32), V((c.R, c.F), F32),
        V((NX, NQ, 128), F32), V((NX, NQ, 128), F32), V((NQ, NX, 128), F32), V((NQ, NX, 128), F32),
        V((NQ, NX, 128), F32), V((NQ, NX, 128), F32), V((NX, NQ, 128), F32), V((NX, NQ, 128), F32),
        V((c.KG, TOK, c.NN), BF), V((c.KG, TOK, 128), BF),
        dma((3,)), dma((4,)), dma((4,)),
        dma((NS,)), dma((NS, 2, c.NH)), dma((NS, 2)), dma((NS, 2)), dma((NS,)), dma((NS,)),
        dma((NS,)), dma((NS,)), dma((NS, 2)), dma((NS, 2)), dma((NS, 2)), dma((NS, 2, c.NH)),
    ]
    vm = pl.BlockSpec(memory_space=pltpu.VMEM)
    hbm = pl.BlockSpec(memory_space=pl.ANY)
    flops = 2 * c.R * c.D * c.F * 6
    return pl.pallas_call(
        functools.partial(kernel, c, order),
        out_shape=(jax.ShapeDtypeStruct((TOK, c.D), BF), jax.ShapeDtypeStruct((TOK, c.D), BF),
                   jax.ShapeDtypeStruct((TOK, c.TOP), BF)),
        in_specs=[vm] * 6 + [hbm] * 3,
        out_specs=(vm, vm, vm),
        scratch_shapes=scratch,
        compiler_params=pltpu.CompilerParams(collective_id=0, has_side_effects=True, vmem_limit_bytes=60 * 2**20),
        cost_estimate=pl.CostEstimate(flops=flops, bytes_accessed=4 * 2**20, transcendentals=c.R * c.F),
        name="expert_layer",
    )(x, dy, fac, perm, cho, quota.reshape(1, NL), wg, wu, wd)


def solution(mesh, **over):
    def step(x, dy, fac, perm, cho, quota, wg, wu, wd):
        c = config(mesh, x.shape[0], perm.shape[1], cho.shape[1], x.shape[1], wg.shape[2], **over)
        return per_device(c, x, dy, fac, perm, cho, quota, wg, wu, wd)

    rows = P(("node", "local"), None)
    cube = P(("node", "local"), None, None)
    return jax.shard_map(
        step,
        mesh=mesh,
        in_specs=(rows, rows, rows, rows, rows, P("node"), cube, cube, cube),
        out_specs=(rows, rows, rows),
        check_vma=False,
    )
```

```python
import functools
import math
from types import SimpleNamespace

import jax
import jax.numpy as jnp
from jax import lax
from jax.experimental import pallas as pl
from jax.experimental.pallas import tpu as pltpu
from jax.sharding import PartitionSpec as P

MESH = pl.DeviceIdType.MESH
BF = jnp.bfloat16
F32 = jnp.float32


INPUT_CUTS = ((2, 2, 2, 2), (2, 2, 2, 2))
OUTPUT_CUTS = ((2, 2, 2, 2), (2, 2, 2, 2))

ORDER = (
    ("ag", 0, 0), ("ag", 1, 0), ("meta1",), ("ag", 0, 1), ("ag", 1, 1), ("ag", 2, 0), ("ag", 1, 2), ("ag", 0, 2),
    ("ag", 1, 3), ("meta2",), ("ag", 0, 3), ("ag", 2, 2), ("pick",), ("ag", 1, 4), ("ag", 2, 1), ("ag", 0, 4), ("ag",
    1, 5), ("z", 1, 0), ("ag", 1, 6), ("ag", 3, 0), ("z", 0, 0), ("ag", 0, 5), ("ag", 3, 1), ("ag", 0, 6), ("ag", 2,
    3), ("ag", 2, 4), ("z", 1, 1), ("ag", 3, 2), ("rank",), ("ag", 3, 3), ("ag", 4, 0), ("z", 0, 1), ("ag", 2, 6),
    ("ag", 2, 5), ("z", 2, 0), ("ag", 4, 1), ("ag", 3, 4), ("y", 1), ("ag", 4, 2), ("ag", 3, 5), ("z", 2, 1), ("z", 3,
    0), ("ag", 4, 3), ("ag", 3, 6), ("y", 0), ("ag", 4, 4), ("ag", 5, 1), ("ag", 4, 5), ("ag", 7, 0), ("z", 3, 1),
    ("ag", 4, 6), ("ag", 5, 0), ("z", 4, 0), ("ag", 6, 1), ("y", 2), ("ag", 6, 0), ("ag", 7, 1), ("z", 4, 1), ("ag",
    5, 3), ("ag", 5, 2), ("ag", 7, 2), ("e", 0), ("ag", 6, 2), ("y", 3), ("ag", 6, 3), ("ag", 7, 3), ("ag", 5, 5),
    ("e", 1), ("ag", 5, 4), ("z", 5, 0), ("ag", 7, 4), ("y", 4), ("ag", 7, 5), ("ag", 6, 4), ("z", 7, 0), ("e", 2),
    ("ag", 5, 6), ("z", 6, 0), ("ag", 7, 6), ("ag", 6, 5), ("e", 3), ("b", 1), ("z", 5, 1), ("ag", 6, 6), ("b", 2),
    ("z", 7, 1), ("b", 3), ("z", 6, 1), ("e", 4), ("m", 1, 1), ("m", 1, 0), ("y", 7), ("y", 5), ("m", 2, 1), ("p", 1,
    1), ("rs", 1, 0), ("m", 3, 1), ("rs", 1, 1), ("m", 2, 0), ("rs", 1, 2), ("p", 2, 1), ("y", 6), ("rs", 2, 0), ("m",
    3, 0), ("rs", 2, 1), ("p", 1, 0), ("b", 0), ("rs", 1, 3), ("p", 3, 1), ("rs", 3, 0), ("rs", 1, 4), ("rs", 3, 1),
    ("rs", 2, 2), ("rs", 1, 5), ("p", 3, 0), ("p", 2, 0), ("rs", 2, 3), ("rs", 3, 2), ("rs", 1, 6), ("rs", 2, 4),
    ("e", 5), ("rs", 3, 3), ("e", 6), ("e", 7), ("b", 4), ("rs", 3, 4), ("rs", 2, 5), ("rs", 2, 6), ("m", 0, 1), ("b",
    7), ("rs", 3, 5), ("m", 0, 0), ("b", 5), ("rs", 3, 6), ("fin", 1), ("m", 4, 1), ("c1",), ("m", 4, 0), ("b", 6),
    ("p", 0, 1), ("rs", 0, 0), ("rs", 0, 1), ("fin", 3), ("m", 7, 1), ("p", 4, 1), ("rs", 4, 0), ("rs", 0, 2), ("rs",
    4, 1), ("p", 0, 0), ("rs", 0, 3), ("c2",), ("m", 5, 1), ("rs", 0, 4), ("m", 7, 0), ("p", 4, 0), ("rs", 4, 2),
    ("p", 7, 1), ("rs", 7, 0), ("rs", 7, 1), ("rs", 4, 3), ("m", 6, 1), ("rs", 0, 5), ("m", 5, 0), ("p", 5, 1), ("rs",
    5, 0), ("rs", 5, 1), ("rs", 7, 2), ("m", 6, 0), ("rs", 4, 4), ("rs", 0, 6), ("rs", 4, 5), ("p", 7, 0), ("rs", 5,
    2), ("p", 6, 1), ("rs", 6, 0), ("rs", 7, 3), ("rs", 6, 1), ("rs", 7, 4), ("p", 5, 0), ("rs", 5, 3), ("rs", 6, 2),
    ("rs", 5, 4), ("fin", 0), ("p", 6, 0), ("rs", 6, 3), ("c3",), ("rs", 4, 6), ("rs", 7, 5), ("rs", 6, 4), ("fin",
    2), ("rs", 7, 6), ("rs", 5, 5), ("rs", 5, 6), ("rs", 6, 5), ("rs", 6, 6), ("fin", 4), ("fin", 7), ("fin", 5),
    ("fin", 6),
)


def cut_columns(unit, cuts):
    streams = []
    for tensor, parts in enumerate(cuts):
        first = 0
        for part in parts:
            streams.append((tensor, first, part * unit))
            first += part * unit
    return streams


def config(mesh, tok, kg, top, feature, hidden, most=12, quota=48):
    c = SimpleNamespace()
    c.NN, c.NL = mesh.shape["node"], mesh.shape["local"]
    c.NX = 8 if c.NN == 64 else 4
    c.NQ = c.NN // c.NX
    c.PC = c.NX // 2
    c.D2 = c.NX // 2
    c.NH = c.NX - 1
    c.TOK, c.KG, c.TOP, c.D, c.F = tok, kg, top, feature, hidden
    c.J, c.Q = most, quota
    unit = feature // 8
    c.inp = cut_columns(unit, INPUT_CUTS)
    c.out = cut_columns(unit, OUTPUT_CUTS)
    c.last = [max(s for s, (n, _, _) in enumerate(c.inp) if n == t) for t in range(2)]
    c.BL = c.PC * c.J
    c.I = 2 * c.NQ * c.BL
    c.R = c.NL * c.Q
    c.H = tok // 2
    return c


def ring_steps(c):
    right, left = [], []
    for d in range(1, c.D2):
        right += [(d, 0), (d, 1)]
        left += [(d, 1), (d, 0)]
    return right + [(c.D2, 0)], left + [(c.D2, 1)]


def slot_of(c, d, side):
    if d == 0:
        return 0
    return 2 * d - 1 if (side == 0 or d == c.D2) else 2 * d


def plan(c, prio=None, gate=(2, 4)):
    NH = c.NH
    prio = prio or {}
    tasks, links = {}, {}
    hop, back, side, across = 2.0, 2.5, 3.5, 2.5

    def add(key, pri, cost, deps, sends=()):
        tasks[key] = (pri + prio.get(key, prio.get(key[0], 0)), cost, deps, sends)

    add(("meta1",), -9, 0.6, [], [(("M1",), "z", 0.2, hop + 1)])
    add(("meta2",), -8, 0.3, [("M1",)], [(("M2",), "x", 0.2, side)])
    add(("pick",), -7, 0.6, [("meta2",)])
    add(("rank",), -6, 1.6, [("M2",)])
    near = 3 if c.D2 > 2 else NH - 1
    for s, (t, _, width) in enumerate(c.inp):
        f = width / c.D
        for h in range(NH):
            start = min(gate[0 if c.inp[s - 1][2] < c.D // 2 else 1], NH - 1)
            deps = [("AG", s, h - 2)] if h >= 2 else ([("ag", s - 1, start)] if s else [])
            add(("ag", s, h), s * 10 - 100, 0.15, deps, [(("AG", s, h), "z", 2.92 * f, hop)])
        for ch in range(2):
            deps = [("pick",)] + [("AG", s, g) for g in range((near if ch == 0 else NH - 1) + 1)]
            add(("z", s, ch), s * 10 + ch, 0.2 + 0.25 * f, deps, [(("Z", s, ch), "x", 9.2 * f, side)])
        add(("y", s), s * 10 + 3, 0.2 + 0.6 * f, [("rank",), ("Z", s, 0), ("Z", s, 1)], [(("Y", s), "y", 18.4 * f, across)])
        deps = [("Y", s)] + ([("e", s - 1)] if s else [])
        add(("e", s), s * 10 + 4, 0.1 + 0.6 * f + (0.5 if s in c.last else 0), deps)
    for u, (t, _, width) in enumerate(c.out):
        f = width / c.D
        at = u * 10 + 4
        add(("b", u), at + 0.5, 0.2 + 0.6 * f, [("e", c.last[t])], [(("B", u), "y", 18.4 * f, across)])
        for ch in (1, 0):
            add(("m", u, ch), at + 1 - ch, 0.15 + 0.3 * f, [("B", u)], [(("RZ", u, ch), "x", 9.2 * f, side)])
            add(("p", u, ch), at + 3 - ch, 0.1 + 0.4 * f, [("RZ", u, ch)])
        for h in range(NH):
            deps = [("p", u, 1)] + ([("p", u, 0)] if h > (2 if c.D2 > 2 else 0) else [])
            deps += [("RS", u, h - 2)] if h >= 2 else []
            add(("rs", u, h), u * 10 - 90, 0.15, deps, [(("RS", u, h), "z", 2.92 * f, back)])
        add(("fin", u), at + 4, 0.2, [("p", u, 0), ("RS", u, NH - 1), ("RS", u, NH - 2)])
    mixes = [u for u, (t, _, _) in enumerate(c.out) if t == 0]
    add(("c1",), 25, 0.6, [("m", u, 0) for u in mixes] + [("y", s) for s, (t, _, _) in enumerate(c.inp) if t], [(("C1",), "x", 0.2, side)])
    add(("c2",), 26, 0.2, [("C1",)], [(("C2",), "z", 0.2, hop + 1)])
    add(("c3",), 27, 0.4, [("C2",)])

    done, now, order = {}, 0.0, []
    left = dict(tasks)
    while left:
        best = None
        for key, (pri, cost, deps, sends) in left.items():
            if any(d not in done for d in deps):
                continue
            at = max([done[d] for d in deps], default=0.0)
            rank = (max(at, now), pri, key)
            if best is None or rank < best[0]:
                best = (rank, key)
        key = best[1]
        pri, cost, deps, sends = left.pop(key)
        now = best[0][0] + cost
        done[key] = now
        for event, link, length, lat in sends:
            start = max(now, links.get(link, 0.0))
            links[link] = start + length
            done[event] = start + length + lat
        order.append(key)
    return order, now


def iota(shape, dim):
    return lax.broadcasted_iota(jnp.int32, shape, dim)


def idiv(v, d):
    if d & (d - 1) == 0:
        return lax.shift_right_logical(v, jnp.int32(d.bit_length() - 1)) if d > 1 else v
    return ((v.astype(F32) + 0.5) * (1.0 / d)).astype(jnp.int32)


def imod(v, d):
    if d & (d - 1) == 0:
        return v & (d - 1)
    return v - idiv(v, d) * d


def onehot(mask):
    return jnp.where(mask, 1.0, 0.0).astype(BF)


def mm(a, b):
    return lax.dot_general(a, b, (((1,), (0,)), ((), ())), preferred_element_type=F32)


def mm_nt(a, b):
    return lax.dot_general(a, b, (((1,), (1,)), ((), ())), preferred_element_type=F32)


def kernel(c, order, x_ref, dy_ref, fac_ref, perm_ref, cho_ref, quota_ref, wg_hbm, wu_hbm, wd_hbm,
           mixed_ref, igrad_ref, coef_ref, *scratch):
    NX, NQ, NL, PC, J, Q, TOK = c.NX, c.NQ, c.NL, c.PC, c.J, c.Q, c.TOK
    NG, I, R, BL = c.NN, c.I, c.R, c.BL
    NI, NO = len(c.inp), len(c.out)
    refs = list(scratch)

    def take(n):
        return [refs.pop(0) for _ in range(n)]

    xg, zs, zr, ys, yr = [take(NI) for _ in range(5)]
    bs, br, rzs, rzr, part, rss, rsr = [take(NO) for _ in range(7)]
    (wg, wu, wd, pick, pickt, sel, selt, selg, ag, au, bk, hid, g_g, g_u, meta, m1, m2s, m2, cm, c1r, c2s, c2r, acat,
     pmask, cols_ref, w_sem, s_small, r_small, ag_s, ag_r, z_s, z_r, y_s, y_r, b_s, b_r, rz_s, rz_r, rs_s, rs_r) = refs
    LANES = 128
    node, y = lax.axis_index("node"), lax.axis_index("local")
    xx, b_me = lax.div(node, NQ), lax.rem(node, NQ)

    def x_peer(o):
        return lax.rem(xx + (o + NX), NX) * NQ + b_me

    def q_peer(i):
        q = lax.rem(b_me + i, NQ)
        return q, xx * NQ + q

    def y_peer(i):
        return lax.rem(y + i, NL)

    def copy(src, dst, send, recv, to_node, to_local):
        return pltpu.make_async_remote_copy(src_ref=src, dst_ref=dst, send_sem=send, recv_sem=recv,
                                            device_id=(to_node, to_local), device_id_type=MESH)

    def await_recv(like, sem):
        copy(like, like, sem, sem, node, y).wait_recv()

    def await_send(like, sem):
        copy(like, like, sem, sem, node, y).wait_send()

    barrier = pltpu.get_barrier_semaphore()
    for o in range(1, NX):
        pl.semaphore_signal(barrier, inc=1, device_id=(x_peer(o), y), device_id_type=MESH)
    for i in range(1, NQ):
        pl.semaphore_signal(barrier, inc=1, device_id=(q_peer(i)[1], y), device_id_type=MESH)
    for i in range(1, NL):
        pl.semaphore_signal(barrier, inc=1, device_id=(node, y_peer(i)), device_id_type=MESH)

    weights = [pltpu.make_async_copy(h.at[0], v, w_sem.at[n])
               for n, (h, v) in enumerate(((wg_hbm, wg), (wu_hbm, wu), (wd_hbm, wd)))]
    for w in weights:
        w.start()
    for s, (t, first, width) in enumerate(c.inp):
        xg[s][0] = (dy_ref if t else x_ref)[:, first:first + width]
    pl.semaphore_wait(barrier, (NX - 1) + (NQ - 1) + (NL - 1))

    rights, lefts = ring_steps(c)

    def offset_of(p):
        d = lax.shift_right_logical(p + 1, jnp.int32(1))
        return jnp.where((p & 1) == 1, -d, d)

    def static_offset(p):
        d = (p + 1) // 2
        return -d if p % 2 else d

    def do_ag(s, h):
        for side, steps in ((0, rights), (1, lefts)):
            if h >= 2 and (s, h - 2) not in waited:
                d0, h0 = steps[h - 2]
                await_recv(xg[s].at[slot_of(c, d0, side), pl.ds(h0 * c.H, c.H)], ag_r.at[s, side, h - 2])
            d, half = steps[h]
            rows = pl.ds(half * c.H, c.H)
            copy(xg[s].at[slot_of(c, d - 1, side), rows], xg[s].at[slot_of(c, d, side), rows],
                 ag_s.at[s], ag_r.at[s, side, h], x_peer(1 if side == 0 else -1), y).start()

    ag_seen = {s: 0 for s in range(NI)}

    def ag_upto(s, h):
        for g in range(ag_seen[s], h + 1):
            if g + 2 >= c.NH or (("ag", s, g + 2) not in issued):
                for side, steps in ((0, rights), (1, lefts)):
                    d0, h0 = steps[g]
                    await_recv(xg[s].at[slot_of(c, d0, side), pl.ds(h0 * c.H, c.H)], ag_r.at[s, side, g])
                waited.add((s, g))
        ag_seen[s] = max(ag_seen[s], h + 1)

    issued, waited = set(), set()

    def do_meta1():
        table = jnp.concatenate([v[...].astype(F32) for v in (cho_ref, fac_ref, perm_ref)], axis=0).astype(BF)
        eye = onehot(iota((TOK, TOK), 0) == iota((TOK, TOK), 1))
        turned = mm_nt(eye, table)
        cols_ref[...] = turned
        cho, perm = turned.astype(jnp.int32), turned[:, 2 * c.TOP:].astype(jnp.int32)
        fac = turned[:, c.TOP:2 * c.TOP]
        lane = iota((TOK, LANES), 1)
        code = iota((TOK, c.KG * NL), 1)
        table = jnp.zeros((TOK, c.KG * NL), F32)
        for n in range(c.TOP):
            table += jnp.where(cho[:, n:n + 1] == code, fac[:, n:n + 1], 0.0)
        table = table.astype(BF)
        groups = iota((TOK, NG), 1)
        named = []
        for s in range(c.KG):
            g = perm[:, s:s + 1]
            named.append(jnp.where(g == groups, 1.0, 0.0))
        total = sum(named[1:], named[0]).astype(BF)
        lower = onehot(iota((TOK, TOK), 1) < iota((TOK, TOK), 0))
        place = mm(lower, total)
        mark = (iota((TOK, LANES), 0) + 1).astype(F32)
        lane_j = idiv(lane, NL)
        out = jnp.zeros((NG, LANES), F32)
        eye = onehot(iota((NG, NG), 0) == iota((NG, NG), 1))
        for s in range(c.KG):
            p = jnp.sum(named[s] * place, axis=1, keepdims=True).astype(jnp.int32)
            spread = onehot((iota((c.KG * NL, LANES), 0) == s * NL + imod(iota((c.KG * NL, LANES), 1), NL)))
            mine = (lane_j == p) & (lane < J * NL)
            rhs = jnp.where(mine, mm(table, spread), 0.0)
            rhs += jnp.where(lane - J * NL == p, mark, 0.0)
            a = named[s].astype(BF)
            out += mm(mm_nt(eye, a).astype(BF), rhs.astype(BF))
            acat[s] = a
            pmask[s] = onehot(mine)
        meta[...] = out.reshape(NX, NQ, LANES)
        m1[0] = meta[xx]
        for p in range(1, NX):
            to = lax.rem(xx + (NX - static_offset(p)), NX)
            copy(meta.at[to], m1.at[p], s_small.at[0], r_small.at[0], to * NQ + b_me, y).start()

    def do_meta2():
        await_recv(m1.at[pl.ds(0, NX - 1)], r_small.at[0])
        flat = m1[...].reshape(NX * NQ, LANES).astype(BF)
        n = NX * NQ
        row, col = iota((n, n), 0), iota((n, n), 1)
        turn = onehot((imod(row, NX) == idiv(col, NQ)) & (idiv(row, NX) == imod(col, NQ)))
        m2s[...] = mm(turn, flat).reshape(NQ, NX, LANES)
        m2[b_me] = m2s[b_me]
        for i in range(1, NQ):
            q, to = q_peer(i)
            copy(m2s.at[q], m2.at[b_me], s_small.at[1], r_small.at[1], to, y).start()

    def do_pick():
        flat = m1[...].reshape(NX * NQ, LANES).astype(BF)
        C = NQ * BL
        row = iota((C, NX * NQ), 0)
        rq, rp = idiv(row, BL), idiv(imod(row, BL), J)
        lane, lrow = iota((C, LANES), 1), iota((C, LANES), 0)
        rcol = iota((C, 1), 0)
        ccol = iota((1, C), 1)
        for ch in range(2):
            take = onehot((rp + ch * PC) * NQ + rq == iota((C, NX * NQ), 1))
            got = jnp.where(lane == J * NL + imod(lrow, J), mm(take, flat), 0.0)
            down = jnp.sum(got, axis=1, keepdims=True).astype(jnp.int32)
            across = mm_nt(jnp.ones((8, LANES), BF), got.astype(BF))[0:1].astype(jnp.int32)
            down = jnp.where(down > 0, down + TOK * idiv(imod(rcol, BL), J), 0)
            across = jnp.where(across > 0, across + TOK * idiv(imod(ccol, BL), J), 0)
            pick[ch] = onehot(down == iota((C, PC * TOK), 1) + 1)
            pickt[ch] = onehot(across == iota((PC * TOK, C), 0) + 1)

    def slot_rows(v):
        half = NQ * BL
        ch = idiv(v, half)
        rest = v - ch * half
        return idiv(rest, BL) * NX + ch * PC + idiv(imod(rest, BL), J)

    def do_rank():
        await_recv(m2.at[pl.ds(0, NQ - 1)], r_small.at[1])
        n = NQ * NX
        mt = m2[...].reshape(n, LANES)
        lane = iota((n, LANES), 1)
        el = (mt != 0.0) & (lane < J * NL)
        elb = onehot(el)
        l0, l1 = iota((LANES, LANES), 0), iota((LANES, LANES), 1)
        same = (imod(l0, NL) == imod(l1, NL)) & (l0 < J * NL)
        inside = mm(elb, onehot(same & (idiv(l0, NL) < idiv(l1, NL))))
        rows = mm(elb, onehot(same)).astype(BF)

        def number(r):
            b, p = idiv(r, NX), imod(r, NX)
            return ((xx + offset_of(p) + NX) & (NX - 1)) * NQ + b

        before = onehot(number(iota((n, n), 1)) < number(iota((n, n), 0)))
        rank = inside + mm(before, rows)
        ql = jnp.broadcast_to(quota_ref[...].astype(F32), (8, NL)).astype(BF)
        ql = mm(ql, onehot(iota((NL, LANES), 0) == imod(iota((NL, LANES), 1), NL)))[0:1]
        keep = el & (rank < ql)
        rk = jnp.where(keep, rank + 1.0, 0.0).astype(BF)
        gk = jnp.where(keep, mt, 0.0).astype(BF)
        eye = onehot(l0 == l1)
        spread = onehot(iota((n, I), 0) == slot_rows(iota((n, I), 1)))
        mine = (idiv(iota((LANES, I), 0), NL) == imod(iota((LANES, I), 1), J)) & (iota((LANES, I), 0) < J * NL)
        fold = onehot((iota((max(NL, 8), LANES), 0) == imod(iota((max(NL, 8), LANES), 1), NL))
                      & (iota((max(NL, 8), LANES), 1) < J * NL))
        flat = jnp.where(mine, mm(mm_nt(eye, rk).astype(BF), spread), 0.0).astype(BF)
        flat = mm(fold, flat)
        for e in range(NL):
            sel[e] = onehot(flat[e:e + 1] == (iota((Q, I), 0) + 1).astype(F32))
        spread = onehot(slot_rows(iota((I, n), 0)) == iota((I, n), 1))
        mine = (idiv(iota((I, LANES), 1), NL) == imod(iota((I, LANES), 0), J)) & (iota((I, LANES), 1) < J * NL)
        widen = onehot((imod(iota((LANES, R), 0), NL) == idiv(iota((LANES, R), 1), Q)) & (iota((LANES, R), 0) < J * NL))
        flat = mm(jnp.where(mine, mm(spread, rk), 0.0).astype(BF), widen)
        gates = mm(jnp.where(mine, mm(spread, gk), 0.0).astype(BF), widen)
        hit = flat == (imod(iota((I, R), 1), Q) + 1).astype(F32)
        selt[...] = onehot(hit)
        selg[...] = jnp.where(hit, gates, 0.0).astype(BF)

    def do_z(s, ch):
        ag_upto(s, 3 if ch == 0 and c.D2 > 2 else c.NH - 1)
        width = c.inp[s][2]
        rows = xg[s][ch * PC:(ch + 1) * PC].reshape(PC * TOK, width)
        zs[s][ch] = mm(pick[ch], rows).astype(BF).reshape(NQ, BL, width)
        for i in range(1, NQ):
            q, to = q_peer(i)
            copy(zs[s].at[ch, q], zr[s].at[ch, b_me], z_s.at[s, ch], z_r.at[s, ch], to, y).start()
        zr[s][ch, b_me] = zs[s][ch, b_me]

    def do_y(s):
        width = c.inp[s][2]
        for ch in range(2):
            await_recv(zr[s].at[ch, pl.ds(0, NQ - 1)], z_r.at[s, ch])
        ys[s][...] = mm(sel[...].reshape(R, I), zr[s][...].reshape(I, width)).astype(BF).reshape(NL, Q, width)
        for i in range(1, NL):
            to = y_peer(i)
            copy(ys[s].at[to], yr[s].at[y], y_s.at[s], y_r.at[s], node, to).start()
        yr[s][y] = ys[s][y]

    def do_e(s):
        await_recv(yr[s].at[pl.ds(0, NL - 1)], y_r.at[s])
        t, first, width = c.inp[s]
        rows = yr[s][...].reshape(R, width)
        cols = slice(first, first + width)
        if s == 0:
            for w in weights:
                w.wait()
        if t == 0:
            a_g, a_u = mm(rows, wg[cols]), mm(rows, wu[cols])
            if first:
                a_g, a_u = a_g + ag[...], a_u + au[...]
            ag[...], au[...] = a_g, a_u
            if s == c.last[0]:
                hid[...] = (a_g * jax.nn.sigmoid(a_g) * a_u).astype(BF)
        else:
            back = mm_nt(rows, wd[:, cols])
            if first:
                back = back + bk[...]
            bk[...] = back
            if s == c.last[1]:
                a_g, a_u = ag[...], au[...]
                sig = jax.nn.sigmoid(a_g)
                g_g[...] = (back * a_u * sig * (1.0 + a_g * (1.0 - sig))).astype(BF)
                g_u[...] = (back * a_g * sig).astype(BF)

    def do_b(u):
        t, first, width = c.out[u]
        cols = slice(first, first + width)
        if t == 0:
            value = mm(hid[...], wd[:, cols])
        else:
            value = mm_nt(g_g[...], wg[cols]) + mm_nt(g_u[...], wu[cols])
        bs[u][...] = value.astype(BF).reshape(NL, Q, width)
        for i in range(1, NL):
            to = y_peer(i)
            copy(bs[u].at[to], br[u].at[y], b_s.at[u], b_r.at[u], node, to).start()
        br[u][y] = bs[u][y]

    b_seen = set()

    def do_m(u, ch):
        width = c.out[u][2]
        if u not in b_seen:
            b_seen.add(u)
            await_recv(br[u].at[pl.ds(0, NL - 1)], b_r.at[u])
        half = I // 2
        rzs[u][ch] = mm(selg[ch * half:(ch + 1) * half], br[u][...].reshape(R, width)).astype(BF).reshape(NQ, BL, width)
        for i in range(1, NQ):
            q, to = q_peer(i)
            copy(rzs[u].at[ch, q], rzr[u].at[ch, b_me], rz_s.at[u, ch], rz_r.at[u, ch], to, y).start()
        rzr[u][ch, b_me] = rzs[u][ch, b_me]

    def do_p(u, ch):
        width = c.out[u][2]
        await_recv(rzr[u].at[ch, pl.ds(0, NQ - 1)], rz_r.at[u, ch])
        sums = mm(pickt[ch], rzr[u][ch].reshape(NQ * BL, width))
        part[u][ch * PC:(ch + 1) * PC] = sums.reshape(PC, TOK, width)

    def do_rs(u, h):
        for side, steps in ((0, rights), (1, lefts)):
            d, half = steps[c.NH - 1 - h]
            value = part[u][slot_of(c, d, side), half * c.H:(half + 1) * c.H]
            if h >= 2:
                await_recv(rsr[u].at[side, h - 2], rs_r.at[u, side, h - 2])
                value = value + rsr[u][side, h - 2].astype(F32)
            rss[u][side, h] = value.astype(BF)
            copy(rss[u].at[side, h], rsr[u].at[side, h], rs_s.at[u, side], rs_r.at[u, side, h],
                 x_peer(-1 if side == 0 else 1), y).start()

    def do_fin(u):
        t, first, width = c.out[u]
        out = igrad_ref if t else mixed_ref
        values = [part[u][0, v * c.H:(v + 1) * c.H] for v in range(2)]
        for side, steps in ((0, rights), (1, lefts)):
            for h in (c.NH - 2, c.NH - 1):
                await_recv(rsr[u].at[side, h], rs_r.at[u, side, h])
                half = steps[c.NH - 1 - h][1]
                values[half] = values[half] + rsr[u][side, h].astype(F32)
        for v in range(2):
            out[v * c.H:(v + 1) * c.H, first:first + width] = values[v].astype(BF)

    def do_c1():
        cd = jnp.zeros((R, 1), F32)
        for s, (t, first, width) in enumerate(c.inp):
            for u, (v, begin, size) in enumerate(c.out):
                low, high = max(first, begin), min(first + width, begin + size)
                if t == 1 and v == 0 and low < high:
                    up = ys[s][:, :, low - first:high - first].reshape(R, high - low).astype(F32)
                    got = br[u][:, :, low - begin:high - begin].reshape(R, high - low).astype(F32)
                    cd += jnp.sum(up * got, axis=1, keepdims=True)
        spread = jnp.where(idiv(iota((R, LANES), 0), Q) == imod(iota((R, LANES), 1), NL), cd, 0.0).astype(BF)
        got = mm(selt[...], spread)
        mine = (idiv(iota((I, LANES), 1), NL) == imod(iota((I, LANES), 0), J)) & (iota((I, LANES), 1) < J * NL)
        got = jnp.where(mine, got, 0.0).astype(BF)
        n = NQ * NX
        fold = onehot(iota((n, I), 0) == slot_rows(iota((n, I), 1)))
        cm[...] = mm(fold, got).reshape(NQ, NX, LANES)
        c1r[b_me] = cm[b_me]
        for i in range(1, NQ):
            q, to = q_peer(i)
            copy(cm.at[q], c1r.at[b_me], s_small.at[2], r_small.at[2], to, y).start()

    def do_c2():
        await_recv(c1r.at[pl.ds(0, NQ - 1)], r_small.at[2])
        n = NX * NQ
        row, col = iota((n, n), 0), iota((n, n), 1)
        turn = onehot((imod(row, NQ) == idiv(col, NX)) & (idiv(row, NQ) == imod(col, NX)))
        c2s[...] = mm(turn, c1r[...].reshape(n, LANES).astype(BF)).reshape(NX, NQ, LANES)
        c2r[xx] = c2s[0]
        for p in range(1, NX):
            to = lax.rem(xx + (static_offset(p) + NX), NX)
            copy(c2s.at[p], c2r.at[xx], s_small.at[3], r_small.at[3], to * NQ + b_me, y).start()

    def do_c3():
        await_recv(c2r.at[pl.ds(0, NX - 1)], r_small.at[3])
        rows = c2r[...].reshape(NX * NQ, LANES).astype(BF)
        codes = c.KG * NL
        tab = jnp.zeros((TOK, codes), F32)
        for s in range(c.KG):
            mine = mm(acat[s], rows) * pmask[s].astype(F32)
            spread = onehot((iota((codes, LANES), 0) == s * NL + imod(iota((codes, LANES), 1), NL)))
            tab += mm_nt(mine.astype(BF), spread)
        cho = cols_ref[...].astype(jnp.int32)
        code, entry = iota((TOK, codes), 1), iota((TOK, c.TOP), 1)
        out = jnp.zeros((TOK, c.TOP), F32)
        for n in range(c.TOP):
            value = jnp.sum(jnp.where(cho[:, n:n + 1] == code, tab, 0.0), axis=1, keepdims=True)
            out += jnp.where(entry == n, value, 0.0)
        eye = onehot(iota((c.TOP, c.TOP), 0) == iota((c.TOP, c.TOP), 1))
        coef_ref[...] = mm_nt(eye, out.astype(BF)).astype(BF)

    steps = {"ag": do_ag, "z": do_z, "y": do_y, "e": do_e, "b": do_b, "m": do_m, "p": do_p, "rs": do_rs, "fin": do_fin,
             "meta1": do_meta1, "meta2": do_meta2, "pick": do_pick, "rank": do_rank,
             "c1": do_c1, "c2": do_c2, "c3": do_c3}
    for key in order:
        steps[key[0]](*key[1:])
        issued.add(key)

    for n, ref in enumerate((m1.at[pl.ds(0, NX - 1)], m2.at[pl.ds(0, NQ - 1)], c1r.at[pl.ds(0, NQ - 1)],
                             c2r.at[pl.ds(0, NX - 1)])):
        await_send(ref, s_small.at[n])
    for s in range(NI):
        await_send(xg[s].at[pl.ds(0, NX - 1)], ag_s.at[s])
        for ch in range(2):
            await_send(zs[s].at[ch, pl.ds(0, NQ - 1)], z_s.at[s, ch])
        await_send(ys[s].at[pl.ds(0, NL - 1)], y_s.at[s])
    for u in range(NO):
        for ch in range(2):
            await_send(rzs[u].at[ch, pl.ds(0, NQ - 1)], rz_s.at[u, ch])
        await_send(bs[u].at[pl.ds(0, NL - 1)], b_s.at[u])
        for side in range(2):
            await_send(rss[u].at[side], rs_s.at[u, side])


def per_device(c, x, dy, fac, perm, cho, quota, wg, wu, wd):
    NX, NQ, NL, PC, Q, TOK = c.NX, c.NQ, c.NL, c.PC, c.Q, c.TOK
    NI, NO = len(c.inp), len(c.out)
    order = ORDER if c.NX == 8 else plan(c)[0]
    dma = pltpu.SemaphoreType.DMA
    V = pltpu.VMEM
    C = NQ * c.BL
    scratch = []
    for lead, kind, streams in (
        ((NX, TOK), BF, c.inp), ((2, NQ, c.BL), BF, c.inp), ((2, NQ, c.BL), BF, c.inp), ((NL, Q), BF, c.inp), ((NL, Q), BF, c.inp),
        ((NL, Q), BF, c.out), ((NL, Q), BF, c.out), ((2, NQ, c.BL), BF, c.out), ((2, NQ, c.BL), BF, c.out),
        ((NX, TOK), F32, c.out), ((2, c.NH, c.H), BF, c.out), ((2, c.NH, c.H), BF, c.out),
    ):
        scratch += [V(lead + (width,), kind) for _, _, width in streams]
    scratch += [
        V((c.D, c.F), BF), V((c.D, c.F), BF), V((c.F, c.D), BF),
        V((2, C, PC * TOK), BF), V((2, PC * TOK, C), BF),
        V((NL, Q, c.I), BF), V((c.I, c.R), BF), V((c.I, c.R), BF),
        V((c.R, c.F), F32), V((c.R, c.F), F32), V((c.R, c.F), F32), V((c.R, c.F), BF), V((c.R, c.F), BF), V((c.R, c.F), BF),
        V((NX, NQ, 128), F32), V((NX, NQ, 128), F32), V((NQ, NX, 128), F32), V((NQ, NX, 128), F32),
        V((NQ, NX, 128), F32), V((NQ, NX, 128), F32), V((NX, NQ, 128), F32), V((NX, NQ, 128), F32),
        V((c.KG, TOK, c.NN), BF), V((c.KG, TOK, 128), BF), V((TOK, 2 * c.TOP + c.KG), F32),
        dma((3,)), dma((4,)), dma((4,)),
        dma((NI,)), dma((NI, 2, c.NH)), dma((NI, 2)), dma((NI, 2)), dma((NI,)), dma((NI,)),
        dma((NO,)), dma((NO,)), dma((NO, 2)), dma((NO, 2)), dma((NO, 2)), dma((NO, 2, c.NH)),
    ]
    vm = pl.BlockSpec(memory_space=pltpu.VMEM)
    hbm = pl.BlockSpec(memory_space=pl.ANY)
    flops = 2 * c.R * c.D * c.F * 6
    mixed, grads, coef = pl.pallas_call(
        functools.partial(kernel, c, order),
        out_shape=(jax.ShapeDtypeStruct((TOK, c.D), BF), jax.ShapeDtypeStruct((TOK, c.D), BF),
                   jax.ShapeDtypeStruct((c.TOP, TOK), BF)),
        in_specs=[vm] * 6 + [hbm] * 3,
        out_specs=(vm, vm, vm),
        scratch_shapes=scratch,
        compiler_params=pltpu.CompilerParams(collective_id=0, has_side_effects=True, vmem_limit_bytes=60 * 2**20),
        cost_estimate=pl.CostEstimate(flops=flops, bytes_accessed=4 * 2**20, transcendentals=c.R * c.F),
        name="expert_layer",
    )(x, dy, fac.T, perm.T, cho.T, quota.reshape(1, NL), wg, wu, wd)
    return mixed, grads, coef.T


def solution(mesh, **over):
    def step(x, dy, fac, perm, cho, quota, wg, wu, wd):
        c = config(mesh, x.shape[0], perm.shape[1], cho.shape[1], x.shape[1], wg.shape[2], **over)
        return per_device(c, x, dy, fac, perm, cho, quota, wg, wu, wd)

    rows = P(("node", "local"), None)
    cube = P(("node", "local"), None, None)
    return jax.shard_map(
        step,
        mesh=mesh,
        in_specs=(rows, rows, rows, rows, rows, P("node"), cube, cube, cube),
        out_specs=(rows, rows, rows),
        check_vma=False,
    )
```

```python
import functools
import math
from types import SimpleNamespace

import jax
import jax.numpy as jnp
from jax import lax
from jax.experimental import pallas as pl
from jax.experimental.pallas import tpu as pltpu
from jax.sharding import PartitionSpec as P

MESH = pl.DeviceIdType.MESH
BF = jnp.bfloat16
F32 = jnp.float32


INPUT_CUTS = ((2, 2, 2, 2), (2, 2, 4))
OUTPUT_CUTS = ((2, 2, 4), (2, 2, 2, 2))

ORDER = (
    ("ag", 0, 0), ("ag", 2, 0), ("meta1",), ("ag", 1, 1), ("ag", 0, 1), ("ag", 0, 2), ("ag", 2, 1), ("ag", 1, 0),
    ("ag", 0, 3), ("ag", 2, 2), ("ag", 0, 4), ("meta2",), ("ag", 3, 0), ("pick",), ("ag", 2, 3), ("ag", 1, 2), ("ag",
    0, 5), ("z", 0, 0), ("ag", 2, 4), ("ag", 0, 6), ("ag", 1, 3), ("z", 2, 0), ("ag", 3, 2), ("ag", 1, 4), ("ag", 3,
    1), ("ag", 2, 6), ("ag", 2, 5), ("ag", 4, 0), ("z", 0, 1), ("rank",), ("z", 1, 0), ("ag", 1, 5), ("ag", 3, 4),
    ("ag", 1, 6), ("ag", 3, 3), ("z", 2, 1), ("ag", 4, 1), ("ag", 4, 2), ("y", 0), ("ag", 3, 6), ("z", 1, 1), ("ag",
    3, 5), ("z", 3, 0), ("ag", 4, 4), ("ag", 4, 3), ("ag", 5, 1), ("ag", 5, 0), ("y", 2), ("z", 3, 1), ("ag", 4, 6),
    ("z", 4, 0), ("ag", 4, 5), ("ag", 6, 1), ("ag", 5, 3), ("ag", 6, 0), ("y", 1), ("z", 4, 1), ("ag", 5, 2), ("y",
    3), ("ag", 6, 3), ("ag", 6, 2), ("e", 0), ("ag", 5, 4), ("z", 5, 0), ("ag", 5, 5), ("e", 1), ("y", 4), ("ag", 6,
    4), ("z", 6, 0), ("ag", 5, 6), ("e", 2), ("ag", 6, 5), ("e", 3), ("b", 0), ("ag", 6, 6), ("z", 5, 1), ("b", 2),
    ("z", 6, 1), ("m", 0, 1), ("y", 5), ("m", 0, 0), ("e", 4), ("y", 6), ("p", 0, 1), ("rs", 0, 0), ("rs", 0, 1),
    ("m", 2, 1), ("rs", 0, 2), ("m", 2, 0), ("p", 0, 0), ("rs", 0, 3), ("rs", 0, 4), ("b", 1), ("p", 2, 1), ("rs", 2,
    0), ("rs", 2, 1), ("rs", 0, 6), ("rs", 0, 5), ("e", 5), ("e", 6), ("b", 6), ("p", 2, 0), ("rs", 2, 2), ("rs", 2,
    3), ("m", 1, 1), ("m", 1, 0), ("b", 3), ("rs", 2, 4), ("c1",), ("rs", 2, 5), ("m", 6, 1), ("b", 5), ("m", 6, 0),
    ("p", 1, 1), ("rs", 1, 0), ("rs", 1, 1), ("b", 4), ("rs", 2, 6), ("m", 3, 1), ("rs", 1, 2), ("p", 1, 0), ("c2",),
    ("p", 6, 1), ("rs", 6, 0), ("m", 3, 0), ("rs", 6, 1), ("rs", 1, 3), ("fin", 2), ("fin", 0), ("m", 5, 1), ("rs", 1,
    4), ("rs", 6, 2), ("p", 3, 1), ("rs", 3, 1), ("rs", 3, 0), ("p", 6, 0), ("rs", 6, 3), ("m", 4, 1), ("rs", 1, 5),
    ("m", 5, 0), ("rs", 1, 6), ("c3",), ("rs", 6, 4), ("m", 4, 0), ("p", 3, 0), ("rs", 3, 3), ("p", 5, 1), ("rs", 5,
    0), ("rs", 5, 1), ("rs", 3, 2), ("p", 4, 1), ("rs", 4, 0), ("rs", 4, 1), ("rs", 6, 6), ("rs", 6, 5), ("fin", 1),
    ("rs", 5, 2), ("rs", 4, 2), ("p", 5, 0), ("rs", 5, 3), ("p", 4, 0), ("rs", 3, 4), ("rs", 4, 3), ("rs", 5, 4),
    ("rs", 4, 4), ("rs", 3, 5), ("rs", 3, 6), ("rs", 5, 5), ("rs", 5, 6), ("rs", 4, 5), ("rs", 4, 6), ("fin", 3),
    ("fin", 6), ("fin", 5), ("fin", 4),
)


def cut_columns(unit, cuts):
    streams = []
    for tensor, parts in enumerate(cuts):
        first = 0
        for part in parts:
            streams.append((tensor, first, part * unit))
            first += part * unit
    return streams


def config(mesh, tok, kg, top, feature, hidden, most=12, quota=48):
    c = SimpleNamespace()
    c.NN, c.NL = mesh.shape["node"], mesh.shape["local"]
    c.NX = 8 if c.NN == 64 else 4
    c.NQ = c.NN // c.NX
    c.PC = c.NX // 2
    c.D2 = c.NX // 2
    c.NH = c.NX - 1
    c.TOK, c.KG, c.TOP, c.D, c.F = tok, kg, top, feature, hidden
    c.J, c.Q = most, quota
    unit = feature // 8
    c.inp = cut_columns(unit, INPUT_CUTS)
    c.out = cut_columns(unit, OUTPUT_CUTS)
    c.last = [max(s for s, (n, _, _) in enumerate(c.inp) if n == t) for t in range(2)]
    c.BL = c.PC * c.J
    c.I = 2 * c.NQ * c.BL
    c.R = c.NL * c.Q
    c.H = tok // 2
    return c


def ring_steps(c):
    right, left = [], []
    for d in range(1, c.D2):
        right += [(d, 0), (d, 1)]
        left += [(d, 1), (d, 0)]
    return right + [(c.D2, 0)], left + [(c.D2, 1)]


def slot_of(c, d, side):
    if d == 0:
        return 0
    return 2 * d - 1 if (side == 0 or d == c.D2) else 2 * d


def plan(c, prio=None, gate=(2, 4)):
    NH = c.NH
    prio = prio or {}
    tasks, links = {}, {}
    hop, back, side, across = 2.0, 2.5, 3.5, 2.5

    def add(key, pri, cost, deps, sends=()):
        tasks[key] = (pri + prio.get(key, prio.get(key[0], 0)), cost, deps, sends)

    add(("meta1",), -9, 0.6, [], [(("M1",), "z", 0.2, hop + 1)])
    add(("meta2",), -8, 0.3, [("M1",)], [(("M2",), "x", 0.2, side)])
    add(("pick",), -7, 0.6, [("meta2",)])
    add(("rank",), -6, 1.6, [("M2",)])
    near = 3 if c.D2 > 2 else NH - 1
    for s, (t, _, width) in enumerate(c.inp):
        f = width / c.D
        for h in range(NH):
            start = min(gate[0 if c.inp[s - 1][2] < c.D // 2 else 1], NH - 1)
            deps = [("AG", s, h - 2)] if h >= 2 else ([("ag", s - 1, start)] if s else [])
            add(("ag", s, h), s * 10 - 100, 0.15, deps, [(("AG", s, h), "z", 2.92 * f, hop)])
        for ch in range(2):
            deps = [("pick",)] + [("AG", s, g) for g in range((near if ch == 0 else NH - 1) + 1)]
            add(("z", s, ch), s * 10 + ch, 0.2 + 0.25 * f, deps, [(("Z", s, ch), "x", 9.2 * f, side)])
        add(("y", s), s * 10 + 3, 0.2 + 0.6 * f, [("rank",), ("Z", s, 0), ("Z", s, 1)], [(("Y", s), "y", 18.4 * f, across)])
        deps = [("Y", s)] + ([("e", s - 1)] if s else [])
        add(("e", s), s * 10 + 4, 0.1 + 0.6 * f + (0.5 if s in c.last else 0), deps)
    for u, (t, _, width) in enumerate(c.out):
        f = width / c.D
        at = u * 10 + 4
        add(("b", u), at + 0.5, 0.2 + 0.6 * f, [("e", c.last[t])], [(("B", u), "y", 18.4 * f, across)])
        for ch in (1, 0):
            add(("m", u, ch), at + 1 - ch, 0.15 + 0.3 * f, [("B", u)], [(("RZ", u, ch), "x", 9.2 * f, side)])
            add(("p", u, ch), at + 3 - ch, 0.1 + 0.4 * f, [("RZ", u, ch)])
        for h in range(NH):
            deps = [("p", u, 1)] + ([("p", u, 0)] if h > (2 if c.D2 > 2 else 0) else [])
            deps += [("RS", u, h - 2)] if h >= 2 else []
            add(("rs", u, h), u * 10 - 90, 0.15, deps, [(("RS", u, h), "z", 2.92 * f, back)])
        add(("fin", u), at + 4, 0.2, [("p", u, 0), ("RS", u, NH - 1), ("RS", u, NH - 2)])
    mixes = [u for u, (t, _, _) in enumerate(c.out) if t == 0]
    add(("c1",), 25, 0.6, [("m", u, 0) for u in mixes] + [("y", s) for s, (t, _, _) in enumerate(c.inp) if t], [(("C1",), "x", 0.2, side)])
    add(("c2",), 26, 0.2, [("C1",)], [(("C2",), "z", 0.2, hop + 1)])
    add(("c3",), 27, 0.4, [("C2",)])

    done, now, order = {}, 0.0, []
    left = dict(tasks)
    while left:
        best = None
        for key, (pri, cost, deps, sends) in left.items():
            if any(d not in done for d in deps):
                continue
            at = max([done[d] for d in deps], default=0.0)
            rank = (max(at, now), pri, key)
            if best is None or rank < best[0]:
                best = (rank, key)
        key = best[1]
        pri, cost, deps, sends = left.pop(key)
        now = best[0][0] + cost
        done[key] = now
        for event, link, length, lat in sends:
            start = max(now, links.get(link, 0.0))
            links[link] = start + length
            done[event] = start + length + lat
        order.append(key)
    return order, now


def iota(shape, dim):
    return lax.broadcasted_iota(jnp.int32, shape, dim)


def idiv(v, d):
    if d & (d - 1) == 0:
        return lax.shift_right_logical(v, jnp.int32(d.bit_length() - 1)) if d > 1 else v
    return ((v.astype(F32) + 0.5) * (1.0 / d)).astype(jnp.int32)


def imod(v, d):
    if d & (d - 1) == 0:
        return v & (d - 1)
    return v - idiv(v, d) * d


def onehot(mask):
    return jnp.where(mask, 1.0, 0.0).astype(BF)


def mm(a, b):
    return lax.dot_general(a, b, (((1,), (0,)), ((), ())), preferred_element_type=F32)


def mm_nt(a, b):
    return lax.dot_general(a, b, (((1,), (1,)), ((), ())), preferred_element_type=F32)


def kernel(c, order, x_ref, dy_ref, fac_ref, perm_ref, cho_ref, quota_ref, wg_hbm, wu_hbm, wd_hbm,
           mixed_ref, igrad_ref, coef_ref, *scratch):
    NX, NQ, NL, PC, J, Q, TOK = c.NX, c.NQ, c.NL, c.PC, c.J, c.Q, c.TOK
    NG, I, R, BL = c.NN, c.I, c.R, c.BL
    NI, NO = len(c.inp), len(c.out)
    refs = list(scratch)

    def take(n):
        return [refs.pop(0) for _ in range(n)]

    xg, zs, zr, ys, yr = [take(NI) for _ in range(5)]
    bs, br, rzs, rzr, part, rss, rsr = [take(NO) for _ in range(7)]
    (wg, wu, wd, pick, pickt, sel, selt, selg, ag, au, bk, hid, g_g, g_u, meta, m1, m2s, m2, cm, c1r, c2s, c2r, acat,
     pmask, cols_ref, w_sem, s_small, r_small, ag_s, ag_r, z_s, z_r, y_s, y_r, b_s, b_r, rz_s, rz_r, rs_s, rs_r) = refs
    LANES = 128
    node, y = lax.axis_index("node"), lax.axis_index("local")
    xx, b_me = lax.div(node, NQ), lax.rem(node, NQ)

    def x_peer(o):
        return lax.rem(xx + (o + NX), NX) * NQ + b_me

    def q_peer(i):
        q = lax.rem(b_me + i, NQ)
        return q, xx * NQ + q

    def y_peer(i):
        return lax.rem(y + i, NL)

    def copy(src, dst, send, recv, to_node, to_local):
        return pltpu.make_async_remote_copy(src_ref=src, dst_ref=dst, send_sem=send, recv_sem=recv,
                                            device_id=(to_node, to_local), device_id_type=MESH)

    def await_recv(like, sem):
        copy(like, like, sem, sem, node, y).wait_recv()

    def await_send(like, sem):
        copy(like, like, sem, sem, node, y).wait_send()

    barrier = pltpu.get_barrier_semaphore()
    for o in range(1, NX):
        pl.semaphore_signal(barrier, inc=1, device_id=(x_peer(o), y), device_id_type=MESH)
    for i in range(1, NQ):
        pl.semaphore_signal(barrier, inc=1, device_id=(q_peer(i)[1], y), device_id_type=MESH)
    for i in range(1, NL):
        pl.semaphore_signal(barrier, inc=1, device_id=(node, y_peer(i)), device_id_type=MESH)

    weights = [pltpu.make_async_copy(h.at[0], v, w_sem.at[n])
               for n, (h, v) in enumerate(((wg_hbm, wg), (wu_hbm, wu), (wd_hbm, wd)))]
    for w in weights:
        w.start()
    for s, (t, first, width) in enumerate(c.inp):
        xg[s][0] = (dy_ref if t else x_ref)[:, first:first + width]
    pl.semaphore_wait(barrier, (NX - 1) + (NQ - 1) + (NL - 1))

    rights, lefts = ring_steps(c)

    def offset_of(p):
        d = lax.shift_right_logical(p + 1, jnp.int32(1))
        return jnp.where((p & 1) == 1, -d, d)

    def static_offset(p):
        d = (p + 1) // 2
        return -d if p % 2 else d

    def do_ag(s, h):
        for side, steps in ((0, rights), (1, lefts)):
            if h >= 2 and (s, h - 2) not in waited:
                d0, h0 = steps[h - 2]
                await_recv(xg[s].at[slot_of(c, d0, side), pl.ds(h0 * c.H, c.H)], ag_r.at[s, side, h - 2])
            d, half = steps[h]
            rows = pl.ds(half * c.H, c.H)
            copy(xg[s].at[slot_of(c, d - 1, side), rows], xg[s].at[slot_of(c, d, side), rows],
                 ag_s.at[s], ag_r.at[s, side, h], x_peer(1 if side == 0 else -1), y).start()

    ag_seen = {s: 0 for s in range(NI)}

    def ag_upto(s, h):
        for g in range(ag_seen[s], h + 1):
            if g + 2 >= c.NH or (("ag", s, g + 2) not in issued):
                for side, steps in ((0, rights), (1, lefts)):
                    d0, h0 = steps[g]
                    await_recv(xg[s].at[slot_of(c, d0, side), pl.ds(h0 * c.H, c.H)], ag_r.at[s, side, g])
                waited.add((s, g))
        ag_seen[s] = max(ag_seen[s], h + 1)

    issued, waited = set(), set()

    def do_meta1():
        table = jnp.concatenate([v[...].astype(F32) for v in (cho_ref, fac_ref, perm_ref)], axis=0).astype(BF)
        eye = onehot(iota((TOK, TOK), 0) == iota((TOK, TOK), 1))
        turned = mm_nt(eye, table)
        cols_ref[...] = turned
        cho, perm = turned.astype(jnp.int32), turned[:, 2 * c.TOP:].astype(jnp.int32)
        fac = turned[:, c.TOP:2 * c.TOP]
        lane = iota((TOK, LANES), 1)
        code = iota((TOK, c.KG * NL), 1)
        table = jnp.zeros((TOK, c.KG * NL), F32)
        for n in range(c.TOP):
            table += jnp.where(cho[:, n:n + 1] == code, fac[:, n:n + 1], 0.0)
        table = table.astype(BF)
        groups = iota((TOK, NG), 1)
        named = []
        for s in range(c.KG):
            g = perm[:, s:s + 1]
            named.append(jnp.where(g == groups, 1.0, 0.0))
        total = sum(named[1:], named[0]).astype(BF)
        lower = onehot(iota((TOK, TOK), 1) < iota((TOK, TOK), 0))
        place = mm(lower, total)
        mark = (iota((TOK, LANES), 0) + 1).astype(F32)
        lane_j = idiv(lane, NL)
        out = jnp.zeros((NG, LANES), F32)
        eye = onehot(iota((NG, NG), 0) == iota((NG, NG), 1))
        for s in range(c.KG):
            p = jnp.sum(named[s] * place, axis=1, keepdims=True).astype(jnp.int32)
            spread = onehot((iota((c.KG * NL, LANES), 0) == s * NL + imod(iota((c.KG * NL, LANES), 1), NL)))
            mine = (lane_j == p) & (lane < J * NL)
            rhs = jnp.where(mine, mm(table, spread), 0.0)
            rhs += jnp.where(lane - J * NL == p, mark, 0.0)
            a = named[s].astype(BF)
            out += mm(mm_nt(eye, a).astype(BF), rhs.astype(BF))
            acat[s] = a
            pmask[s] = onehot(mine)
        meta[...] = out.reshape(NX, NQ, LANES)
        m1[0] = meta[xx]
        for p in range(1, NX):
            to = lax.rem(xx + (NX - static_offset(p)), NX)
            copy(meta.at[to], m1.at[p], s_small.at[0], r_small.at[0], to * NQ + b_me, y).start()

    def do_meta2():
        await_recv(m1.at[pl.ds(0, NX - 1)], r_small.at[0])
        flat = m1[...].reshape(NX * NQ, LANES).astype(BF)
        n = NX * NQ
        row, col = iota((n, n), 0), iota((n, n), 1)
        turn = onehot((imod(row, NX) == idiv(col, NQ)) & (idiv(row, NX) == imod(col, NQ)))
        m2s[...] = mm(turn, flat).reshape(NQ, NX, LANES)
        m2[b_me] = m2s[b_me]
        for i in range(1, NQ):
            q, to = q_peer(i)
            copy(m2s.at[q], m2.at[b_me], s_small.at[1], r_small.at[1], to, y).start()

    def do_pick():
        flat = m1[...].reshape(NX * NQ, LANES).astype(BF)
        C = NQ * BL
        row = iota((C, NX * NQ), 0)
        rq, rp = idiv(row, BL), idiv(imod(row, BL), J)
        lane, lrow = iota((C, LANES), 1), iota((C, LANES), 0)
        rcol = iota((C, 1), 0)
        ccol = iota((1, C), 1)
        for ch in range(2):
            take = onehot((rp + ch * PC) * NQ + rq == iota((C, NX * NQ), 1))
            got = jnp.where(lane == J * NL + imod(lrow, J), mm(take, flat), 0.0)
            down = jnp.sum(got, axis=1, keepdims=True).astype(jnp.int32)
            across = mm_nt(jnp.ones((8, LANES), BF), got.astype(BF))[0:1].astype(jnp.int32)
            down = jnp.where(down > 0, down + TOK * idiv(imod(rcol, BL), J), 0)
            across = jnp.where(across > 0, across + TOK * idiv(imod(ccol, BL), J), 0)
            pick[ch] = onehot(down == iota((C, PC * TOK), 1) + 1)
            pickt[ch] = onehot(across == iota((PC * TOK, C), 0) + 1)

    def slot_rows(v):
        half = NQ * BL
        ch = idiv(v, half)
        rest = v - ch * half
        return idiv(rest, BL) * NX + ch * PC + idiv(imod(rest, BL), J)

    def do_rank():
        await_recv(m2.at[pl.ds(0, NQ - 1)], r_small.at[1])
        n = NQ * NX
        mt = m2[...].reshape(n, LANES)
        lane = iota((n, LANES), 1)
        el = (mt != 0.0) & (lane < J * NL)
        elb = onehot(el)
        l0, l1 = iota((LANES, LANES), 0), iota((LANES, LANES), 1)
        same = (imod(l0, NL) == imod(l1, NL)) & (l0 < J * NL)
        inside = mm(elb, onehot(same & (idiv(l0, NL) < idiv(l1, NL))))
        rows = mm(elb, onehot(same)).astype(BF)

        def number(r):
            b, p = idiv(r, NX), imod(r, NX)
            return ((xx + offset_of(p) + NX) & (NX - 1)) * NQ + b

        before = onehot(number(iota((n, n), 1)) < number(iota((n, n), 0)))
        rank = inside + mm(before, rows)
        ql = jnp.broadcast_to(quota_ref[...].astype(F32), (8, NL)).astype(BF)
        ql = mm(ql, onehot(iota((NL, LANES), 0) == imod(iota((NL, LANES), 1), NL)))[0:1]
        keep = el & (rank < ql)
        rk = jnp.where(keep, rank + 1.0, 0.0).astype(BF)
        gk = jnp.where(keep, mt, 0.0).astype(BF)
        eye = onehot(l0 == l1)
        spread = onehot(iota((n, I), 0) == slot_rows(iota((n, I), 1)))
        mine = (idiv(iota((LANES, I), 0), NL) == imod(iota((LANES, I), 1), J)) & (iota((LANES, I), 0) < J * NL)
        fold = onehot((iota((max(NL, 8), LANES), 0) == imod(iota((max(NL, 8), LANES), 1), NL))
                      & (iota((max(NL, 8), LANES), 1) < J * NL))
        flat = jnp.where(mine, mm(mm_nt(eye, rk).astype(BF), spread), 0.0).astype(BF)
        flat = mm(fold, flat)
        for e in range(NL):
            sel[e] = onehot(flat[e:e + 1] == (iota((Q, I), 0) + 1).astype(F32))
        spread = onehot(slot_rows(iota((I, n), 0)) == iota((I, n), 1))
        mine = (idiv(iota((I, LANES), 1), NL) == imod(iota((I, LANES), 0), J)) & (iota((I, LANES), 1) < J * NL)
        widen = onehot((imod(iota((LANES, R), 0), NL) == idiv(iota((LANES, R), 1), Q)) & (iota((LANES, R), 0) < J * NL))
        flat = mm(jnp.where(mine, mm(spread, rk), 0.0).astype(BF), widen)
        gates = mm(jnp.where(mine, mm(spread, gk), 0.0).astype(BF), widen)
        hit = flat == (imod(iota((I, R), 1), Q) + 1).astype(F32)
        selt[...] = onehot(hit)
        selg[...] = jnp.where(hit, gates, 0.0).astype(BF)

    def do_z(s, ch):
        ag_upto(s, 3 if ch == 0 and c.D2 > 2 else c.NH - 1)
        width = c.inp[s][2]
        rows = xg[s][ch * PC:(ch + 1) * PC].reshape(PC * TOK, width)
        zs[s][ch] = mm(pick[ch], rows).astype(BF).reshape(NQ, BL, width)
        for i in range(1, NQ):
            q, to = q_peer(i)
            copy(zs[s].at[ch, q], zr[s].at[ch, b_me], z_s.at[s, ch], z_r.at[s, ch], to, y).start()
        zr[s][ch, b_me] = zs[s][ch, b_me]

    def do_y(s):
        width = c.inp[s][2]
        for ch in range(2):
            await_recv(zr[s].at[ch, pl.ds(0, NQ - 1)], z_r.at[s, ch])
        ys[s][...] = mm(sel[...].reshape(R, I), zr[s][...].reshape(I, width)).astype(BF).reshape(NL, Q, width)
        for i in range(1, NL):
            to = y_peer(i)
            copy(ys[s].at[to], yr[s].at[y], y_s.at[s], y_r.at[s], node, to).start()
        yr[s][y] = ys[s][y]

    def do_e(s):
        await_recv(yr[s].at[pl.ds(0, NL - 1)], y_r.at[s])
        t, first, width = c.inp[s]
        rows = yr[s][...].reshape(R, width)
        cols = slice(first, first + width)
        if s == 0:
            for w in weights:
                w.wait()
        if t == 0:
            a_g, a_u = mm(rows, wg[cols]), mm(rows, wu[cols])
            if first:
                a_g, a_u = a_g + ag[...], a_u + au[...]
            ag[...], au[...] = a_g, a_u
            if s == c.last[0]:
                hid[...] = (a_g * jax.nn.sigmoid(a_g) * a_u).astype(BF)
        else:
            back = mm_nt(rows, wd[:, cols])
            if first:
                back = back + bk[...]
            bk[...] = back
            if s == c.last[1]:
                a_g, a_u = ag[...], au[...]
                sig = jax.nn.sigmoid(a_g)
                g_g[...] = (back * a_u * sig * (1.0 + a_g * (1.0 - sig))).astype(BF)
                g_u[...] = (back * a_g * sig).astype(BF)

    def do_b(u):
        t, first, width = c.out[u]
        cols = slice(first, first + width)
        if t == 0:
            value = mm(hid[...], wd[:, cols])
        else:
            value = mm_nt(g_g[...], wg[cols]) + mm_nt(g_u[...], wu[cols])
        bs[u][...] = value.astype(BF).reshape(NL, Q, width)
        for i in range(1, NL):
            to = y_peer(i)
            copy(bs[u].at[to], br[u].at[y], b_s.at[u], b_r.at[u], node, to).start()
        br[u][y] = bs[u][y]

    b_seen = set()

    def do_m(u, ch):
        width = c.out[u][2]
        if u not in b_seen:
            b_seen.add(u)
            await_recv(br[u].at[pl.ds(0, NL - 1)], b_r.at[u])
        half = I // 2
        rzs[u][ch] = mm(selg[ch * half:(ch + 1) * half], br[u][...].reshape(R, width)).astype(BF).reshape(NQ, BL, width)
        for i in range(1, NQ):
            q, to = q_peer(i)
            copy(rzs[u].at[ch, q], rzr[u].at[ch, b_me], rz_s.at[u, ch], rz_r.at[u, ch], to, y).start()
        rzr[u][ch, b_me] = rzs[u][ch, b_me]

    def do_p(u, ch):
        width = c.out[u][2]
        await_recv(rzr[u].at[ch, pl.ds(0, NQ - 1)], rz_r.at[u, ch])
        sums = mm(pickt[ch], rzr[u][ch].reshape(NQ * BL, width))
        part[u][ch * PC:(ch + 1) * PC] = sums.reshape(PC, TOK, width)

    def do_rs(u, h):
        for side, steps in ((0, rights), (1, lefts)):
            d, half = steps[c.NH - 1 - h]
            value = part[u][slot_of(c, d, side), half * c.H:(half + 1) * c.H]
            if h >= 2:
                await_recv(rsr[u].at[side, h - 2], rs_r.at[u, side, h - 2])
                value = value + rsr[u][side, h - 2].astype(F32)
            rss[u][side, h] = value.astype(BF)
            copy(rss[u].at[side, h], rsr[u].at[side, h], rs_s.at[u, side], rs_r.at[u, side, h],
                 x_peer(-1 if side == 0 else 1), y).start()

    def do_fin(u):
        t, first, width = c.out[u]
        out = igrad_ref if t else mixed_ref
        values = [part[u][0, v * c.H:(v + 1) * c.H] for v in range(2)]
        for side, steps in ((0, rights), (1, lefts)):
            for h in (c.NH - 2, c.NH - 1):
                await_recv(rsr[u].at[side, h], rs_r.at[u, side, h])
                half = steps[c.NH - 1 - h][1]
                values[half] = values[half] + rsr[u][side, h].astype(F32)
        for v in range(2):
            out[v * c.H:(v + 1) * c.H, first:first + width] = values[v].astype(BF)

    def do_c1():
        cd = jnp.zeros((R, 1), F32)
        for s, (t, first, width) in enumerate(c.inp):
            for u, (v, begin, size) in enumerate(c.out):
                low, high = max(first, begin), min(first + width, begin + size)
                if t == 1 and v == 0 and low < high:
                    up = ys[s][:, :, low - first:high - first].reshape(R, high - low).astype(F32)
                    got = br[u][:, :, low - begin:high - begin].reshape(R, high - low).astype(F32)
                    cd += jnp.sum(up * got, axis=1, keepdims=True)
        spread = jnp.where(idiv(iota((R, LANES), 0), Q) == imod(iota((R, LANES), 1), NL), cd, 0.0).astype(BF)
        got = mm(selt[...], spread)
        mine = (idiv(iota((I, LANES), 1), NL) == imod(iota((I, LANES), 0), J)) & (iota((I, LANES), 1) < J * NL)
        got = jnp.where(mine, got, 0.0).astype(BF)
        n = NQ * NX
        fold = onehot(iota((n, I), 0) == slot_rows(iota((n, I), 1)))
        cm[...] = mm(fold, got).reshape(NQ, NX, LANES)
        c1r[b_me] = cm[b_me]
        for i in range(1, NQ):
            q, to = q_peer(i)
            copy(cm.at[q], c1r.at[b_me], s_small.at[2], r_small.at[2], to, y).start()

    def do_c2():
        await_recv(c1r.at[pl.ds(0, NQ - 1)], r_small.at[2])
        n = NX * NQ
        row, col = iota((n, n), 0), iota((n, n), 1)
        turn = onehot((imod(row, NQ) == idiv(col, NX)) & (idiv(row, NQ) == imod(col, NX)))
        c2s[...] = mm(turn, c1r[...].reshape(n, LANES).astype(BF)).reshape(NX, NQ, LANES)
        c2r[xx] = c2s[0]
        for p in range(1, NX):
            to = lax.rem(xx + (static_offset(p) + NX), NX)
            copy(c2s.at[p], c2r.at[xx], s_small.at[3], r_small.at[3], to * NQ + b_me, y).start()

    def do_c3():
        await_recv(c2r.at[pl.ds(0, NX - 1)], r_small.at[3])
        rows = c2r[...].reshape(NX * NQ, LANES).astype(BF)
        codes = c.KG * NL
        tab = jnp.zeros((TOK, codes), F32)
        for s in range(c.KG):
            mine = mm(acat[s], rows) * pmask[s].astype(F32)
            spread = onehot((iota((codes, LANES), 0) == s * NL + imod(iota((codes, LANES), 1), NL)))
            tab += mm_nt(mine.astype(BF), spread)
        cho = cols_ref[...].astype(jnp.int32)
        code, entry = iota((TOK, codes), 1), iota((TOK, c.TOP), 1)
        out = jnp.zeros((TOK, c.TOP), F32)
        for n in range(c.TOP):
            value = jnp.sum(jnp.where(cho[:, n:n + 1] == code, tab, 0.0), axis=1, keepdims=True)
            out += jnp.where(entry == n, value, 0.0)
        eye = onehot(iota((c.TOP, c.TOP), 0) == iota((c.TOP, c.TOP), 1))
        coef_ref[...] = mm_nt(eye, out.astype(BF)).astype(BF)

    steps = {"ag": do_ag, "z": do_z, "y": do_y, "e": do_e, "b": do_b, "m": do_m, "p": do_p, "rs": do_rs, "fin": do_fin,
             "meta1": do_meta1, "meta2": do_meta2, "pick": do_pick, "rank": do_rank,
             "c1": do_c1, "c2": do_c2, "c3": do_c3}
    for key in order:
        steps[key[0]](*key[1:])
        issued.add(key)

    for n, ref in enumerate((m1.at[pl.ds(0, NX - 1)], m2.at[pl.ds(0, NQ - 1)], c1r.at[pl.ds(0, NQ - 1)],
                             c2r.at[pl.ds(0, NX - 1)])):
        await_send(ref, s_small.at[n])
    for s in range(NI):
        await_send(xg[s].at[pl.ds(0, NX - 1)], ag_s.at[s])
        for ch in range(2):
            await_send(zs[s].at[ch, pl.ds(0, NQ - 1)], z_s.at[s, ch])
        await_send(ys[s].at[pl.ds(0, NL - 1)], y_s.at[s])
    for u in range(NO):
        for ch in range(2):
            await_send(rzs[u].at[ch, pl.ds(0, NQ - 1)], rz_s.at[u, ch])
        await_send(bs[u].at[pl.ds(0, NL - 1)], b_s.at[u])
        for side in range(2):
            await_send(rss[u].at[side], rs_s.at[u, side])


def per_device(c, x, dy, fac, perm, cho, quota, wg, wu, wd):
    NX, NQ, NL, PC, Q, TOK = c.NX, c.NQ, c.NL, c.PC, c.Q, c.TOK
    NI, NO = len(c.inp), len(c.out)
    order = ORDER if c.NX == 8 else plan(c)[0]
    dma = pltpu.SemaphoreType.DMA
    V = pltpu.VMEM
    C = NQ * c.BL
    scratch = []
    for lead, kind, streams in (
        ((NX, TOK), BF, c.inp), ((2, NQ, c.BL), BF, c.inp), ((2, NQ, c.BL), BF, c.inp), ((NL, Q), BF, c.inp), ((NL, Q), BF, c.inp),
        ((NL, Q), BF, c.out), ((NL, Q), BF, c.out), ((2, NQ, c.BL), BF, c.out), ((2, NQ, c.BL), BF, c.out),
        ((NX, TOK), F32, c.out), ((2, c.NH, c.H), BF, c.out), ((2, c.NH, c.H), BF, c.out),
    ):
        scratch += [V(lead + (width,), kind) for _, _, width in streams]
    scratch += [
        V((c.D, c.F), BF), V((c.D, c.F), BF), V((c.F, c.D), BF),
        V((2, C, PC * TOK), BF), V((2, PC * TOK, C), BF),
        V((NL, Q, c.I), BF), V((c.I, c.R), BF), V((c.I, c.R), BF),
        V((c.R, c.F), F32), V((c.R, c.F), F32), V((c.R, c.F), F32), V((c.R, c.F), BF), V((c.R, c.F), BF), V((c.R, c.F), BF),
        V((NX, NQ, 128), F32), V((NX, NQ, 128), F32), V((NQ, NX, 128), F32), V((NQ, NX, 128), F32),
        V((NQ, NX, 128), F32), V((NQ, NX, 128), F32), V((NX, NQ, 128), F32), V((NX, NQ, 128), F32),
        V((c.KG, TOK, c.NN), BF), V((c.KG, TOK, 128), BF), V((TOK, 2 * c.TOP + c.KG), F32),
        dma((3,)), dma((4,)), dma((4,)),
        dma((NI,)), dma((NI, 2, c.NH)), dma((NI, 2)), dma((NI, 2)), dma((NI,)), dma((NI,)),
        dma((NO,)), dma((NO,)), dma((NO, 2)), dma((NO, 2)), dma((NO, 2)), dma((NO, 2, c.NH)),
    ]
    vm = pl.BlockSpec(memory_space=pltpu.VMEM)
    hbm = pl.BlockSpec(memory_space=pl.ANY)
    flops = 2 * c.R * c.D * c.F * 6
    mixed, grads, coef = pl.pallas_call(
        functools.partial(kernel, c, order),
        out_shape=(jax.ShapeDtypeStruct((TOK, c.D), BF), jax.ShapeDtypeStruct((TOK, c.D), BF),
                   jax.ShapeDtypeStruct((c.TOP, TOK), BF)),
        in_specs=[vm] * 6 + [hbm] * 3,
        out_specs=(vm, vm, vm),
        scratch_shapes=scratch,
        compiler_params=pltpu.CompilerParams(collective_id=0, has_side_effects=True, vmem_limit_bytes=60 * 2**20),
        cost_estimate=pl.CostEstimate(flops=flops, bytes_accessed=4 * 2**20, transcendentals=c.R * c.F),
        name="expert_layer",
    )(x, dy, fac.T, perm.T, cho.T, quota.reshape(1, NL), wg, wu, wd)
    return mixed, grads, coef.T


def solution(mesh, **over):
    def step(x, dy, fac, perm, cho, quota, wg, wu, wd):
        c = config(mesh, x.shape[0], perm.shape[1], cho.shape[1], x.shape[1], wg.shape[2], **over)
        return per_device(c, x, dy, fac, perm, cho, quota, wg, wu, wd)

    rows = P(("node", "local"), None)
    cube = P(("node", "local"), None, None)
    return jax.shard_map(
        step,
        mesh=mesh,
        in_specs=(rows, rows, rows, rows, rows, P("node"), cube, cube, cube),
        out_specs=(rows, rows, rows),
        check_vma=False,
    )
```

```python
import functools
import math
from types import SimpleNamespace

import jax
import jax.numpy as jnp
from jax import lax
from jax.experimental import pallas as pl
from jax.experimental.pallas import tpu as pltpu
from jax.sharding import PartitionSpec as P

MESH = pl.DeviceIdType.MESH
BF = jnp.bfloat16
F32 = jnp.float32


INPUT_CUTS = ((2, 2, 2, 2), (2, 2, 4))
OUTPUT_CUTS = ((2, 2, 4), (2, 2, 2, 2))

ORDER = (
    ("ag", 0, 0), ("ag", 2, 0), ("meta1",), ("ag", 1, 1), ("ag", 0, 1), ("ag", 0, 2), ("ag", 2, 1), ("ag", 1, 0),
    ("ag", 0, 3), ("ag", 2, 2), ("ag", 0, 4), ("meta2",), ("ag", 3, 0), ("pick",), ("ag", 2, 3), ("ag", 1, 2), ("ag",
    0, 5), ("z", 0, 0), ("ag", 2, 4), ("ag", 0, 6), ("ag", 1, 3), ("z", 2, 0), ("ag", 3, 2), ("ag", 1, 4), ("ag", 3,
    1), ("ag", 2, 6), ("ag", 2, 5), ("ag", 4, 0), ("z", 0, 1), ("rank",), ("z", 1, 0), ("ag", 1, 5), ("ag", 3, 4),
    ("ag", 1, 6), ("ag", 3, 3), ("z", 2, 1), ("ag", 4, 1), ("ag", 4, 2), ("y", 0), ("ag", 3, 6), ("z", 1, 1), ("ag",
    3, 5), ("z", 3, 0), ("ag", 4, 4), ("ag", 4, 3), ("ag", 5, 1), ("ag", 5, 0), ("y", 2), ("z", 3, 1), ("ag", 4, 6),
    ("z", 4, 0), ("ag", 4, 5), ("ag", 6, 1), ("ag", 5, 3), ("ag", 6, 0), ("y", 1), ("z", 4, 1), ("ag", 5, 2), ("y",
    3), ("ag", 6, 3), ("ag", 6, 2), ("e", 0), ("ag", 5, 4), ("z", 5, 0), ("ag", 5, 5), ("e", 1), ("y", 4), ("ag", 6,
    4), ("z", 6, 0), ("ag", 5, 6), ("e", 2), ("ag", 6, 5), ("e", 3), ("b", 0), ("ag", 6, 6), ("z", 5, 1), ("b", 2),
    ("z", 6, 1), ("m", 0, 1), ("y", 5), ("m", 0, 0), ("e", 4), ("y", 6), ("p", 0, 1), ("rs", 0, 0), ("rs", 0, 1),
    ("m", 2, 1), ("rs", 0, 2), ("m", 2, 0), ("p", 0, 0), ("rs", 0, 3), ("rs", 0, 4), ("b", 1), ("p", 2, 1), ("rs", 2,
    0), ("rs", 2, 1), ("rs", 0, 6), ("rs", 0, 5), ("e", 5), ("e", 6), ("b", 6), ("p", 2, 0), ("rs", 2, 2), ("rs", 2,
    3), ("m", 1, 1), ("m", 1, 0), ("b", 3), ("rs", 2, 4), ("c1",), ("rs", 2, 5), ("m", 6, 1), ("b", 5), ("m", 6, 0),
    ("p", 1, 1), ("rs", 1, 0), ("rs", 1, 1), ("b", 4), ("rs", 2, 6), ("m", 3, 1), ("rs", 1, 2), ("p", 1, 0), ("c2",),
    ("p", 6, 1), ("rs", 6, 0), ("m", 3, 0), ("rs", 6, 1), ("rs", 1, 3), ("fin", 2), ("fin", 0), ("m", 5, 1), ("rs", 1,
    4), ("rs", 6, 2), ("p", 3, 1), ("rs", 3, 1), ("rs", 3, 0), ("p", 6, 0), ("rs", 6, 3), ("m", 4, 1), ("rs", 1, 5),
    ("m", 5, 0), ("rs", 1, 6), ("c3",), ("rs", 6, 4), ("m", 4, 0), ("p", 3, 0), ("rs", 3, 3), ("p", 5, 1), ("rs", 5,
    0), ("rs", 5, 1), ("rs", 3, 2), ("p", 4, 1), ("rs", 4, 0), ("rs", 4, 1), ("rs", 6, 6), ("rs", 6, 5), ("fin", 1),
    ("rs", 5, 2), ("rs", 4, 2), ("p", 5, 0), ("rs", 5, 3), ("p", 4, 0), ("rs", 3, 4), ("rs", 4, 3), ("rs", 5, 4),
    ("rs", 4, 4), ("rs", 3, 5), ("rs", 3, 6), ("rs", 5, 5), ("rs", 5, 6), ("rs", 4, 5), ("rs", 4, 6), ("fin", 3),
    ("fin", 6), ("fin", 5), ("fin", 4),
)


def cut_columns(unit, cuts):
    streams = []
    for tensor, parts in enumerate(cuts):
        first = 0
        for part in parts:
            streams.append((tensor, first, part * unit))
            first += part * unit
    return streams


def config(mesh, tok, kg, top, feature, hidden, most=12, quota=48):
    c = SimpleNamespace()
    c.NN, c.NL = mesh.shape["node"], mesh.shape["local"]
    c.NX = 8 if c.NN == 64 else 4
    c.NQ = c.NN // c.NX
    c.PC = c.NX // 2
    c.D2 = c.NX // 2
    c.NH = c.NX - 1
    c.TOK, c.KG, c.TOP, c.D, c.F = tok, kg, top, feature, hidden
    c.J, c.Q = most, quota
    unit = feature // 8
    c.inp = cut_columns(unit, INPUT_CUTS)
    c.out = cut_columns(unit, OUTPUT_CUTS)
    c.last = [max(s for s, (n, _, _) in enumerate(c.inp) if n == t) for t in range(2)]
    c.BL = c.PC * c.J
    c.I = 2 * c.NQ * c.BL
    c.R = c.NL * c.Q
    c.H = tok // 2
    return c


def ring_steps(c):
    right, left = [], []
    for d in range(1, c.D2):
        right += [(d, 0), (d, 1)]
        left += [(d, 1), (d, 0)]
    return right + [(c.D2, 0)], left + [(c.D2, 1)]


def slot_of(c, d, side):
    if d == 0:
        return 0
    return 2 * d - 1 if (side == 0 or d == c.D2) else 2 * d


def plan(c, prio=None, gate=(2, 4)):
    NH = c.NH
    prio = prio or {}
    tasks, links = {}, {}
    hop, back, side, across = 2.0, 2.5, 3.5, 2.5

    def add(key, pri, cost, deps, sends=()):
        tasks[key] = (pri + prio.get(key, prio.get(key[0], 0)), cost, deps, sends)

    add(("meta1",), -9, 0.6, [], [(("M1",), "z", 0.2, hop + 1)])
    add(("meta2",), -8, 0.3, [("M1",)], [(("M2",), "x", 0.2, side)])
    add(("pick",), -7, 0.6, [("meta2",)])
    add(("rank",), -6, 1.6, [("M2",)])
    near = 3 if c.D2 > 2 else NH - 1
    for s, (t, _, width) in enumerate(c.inp):
        f = width / c.D
        for h in range(NH):
            start = min(gate[0 if c.inp[s - 1][2] < c.D // 2 else 1], NH - 1)
            deps = [("AG", s, h - 2)] if h >= 2 else ([("ag", s - 1, start)] if s else [])
            add(("ag", s, h), s * 10 - 100, 0.15, deps, [(("AG", s, h), "z", 2.92 * f, hop)])
        for ch in range(2):
            deps = [("pick",)] + [("AG", s, g) for g in range((near if ch == 0 else NH - 1) + 1)]
            add(("z", s, ch), s * 10 + ch, 0.2 + 0.25 * f, deps, [(("Z", s, ch), "x", 9.2 * f, side)])
        add(("y", s), s * 10 + 3, 0.2 + 0.6 * f, [("rank",), ("Z", s, 0), ("Z", s, 1)], [(("Y", s), "y", 18.4 * f, across)])
        deps = [("Y", s)] + ([("e", s - 1)] if s else [])
        add(("e", s), s * 10 + 4, 0.1 + 0.6 * f + (0.5 if s in c.last else 0), deps)
    for u, (t, _, width) in enumerate(c.out):
        f = width / c.D
        at = u * 10 + 4
        add(("b", u), at + 0.5, 0.2 + 0.6 * f, [("e", c.last[t])], [(("B", u), "y", 18.4 * f, across)])
        for ch in (1, 0):
            add(("m", u, ch), at + 1 - ch, 0.15 + 0.3 * f, [("B", u)], [(("RZ", u, ch), "x", 9.2 * f, side)])
            add(("p", u, ch), at + 3 - ch, 0.1 + 0.4 * f, [("RZ", u, ch)])
        for h in range(NH):
            deps = [("p", u, 1)] + ([("p", u, 0)] if h > (2 if c.D2 > 2 else 0) else [])
            deps += [("RS", u, h - 2)] if h >= 2 else []
            add(("rs", u, h), u * 10 - 90, 0.15, deps, [(("RS", u, h), "z", 2.92 * f, back)])
        add(("fin", u), at + 4, 0.2, [("p", u, 0), ("RS", u, NH - 1), ("RS", u, NH - 2)])
    mixes = [u for u, (t, _, _) in enumerate(c.out) if t == 0]
    add(("c1",), 25, 0.6, [("m", u, 0) for u in mixes] + [("y", s) for s, (t, _, _) in enumerate(c.inp) if t], [(("C1",), "x", 0.2, side)])
    add(("c2",), 26, 0.2, [("C1",)], [(("C2",), "z", 0.2, hop + 1)])
    add(("c3",), 27, 0.4, [("C2",)])

    done, now, order = {}, 0.0, []
    left = dict(tasks)
    while left:
        best = None
        for key, (pri, cost, deps, sends) in left.items():
            if any(d not in done for d in deps):
                continue
            at = max([done[d] for d in deps], default=0.0)
            rank = (max(at, now), pri, key)
            if best is None or rank < best[0]:
                best = (rank, key)
        key = best[1]
        pri, cost, deps, sends = left.pop(key)
        now = best[0][0] + cost
        done[key] = now
        for event, link, length, lat in sends:
            start = max(now, links.get(link, 0.0))
            links[link] = start + length
            done[event] = start + length + lat
        order.append(key)
    return order, now


def iota(shape, dim):
    return lax.broadcasted_iota(jnp.int32, shape, dim)


def idiv(v, d):
    if d & (d - 1) == 0:
        return lax.shift_right_logical(v, jnp.int32(d.bit_length() - 1)) if d > 1 else v
    return ((v.astype(F32) + 0.5) * (1.0 / d)).astype(jnp.int32)


def imod(v, d):
    if d & (d - 1) == 0:
        return v & (d - 1)
    return v - idiv(v, d) * d


def far_first(n):
    return sorted(range(1, n), key=lambda i: (-min(i, n - i), i))


def onehot(mask):
    return jnp.where(mask, 1.0, 0.0).astype(BF)


def mm(a, b):
    return lax.dot_general(a, b, (((1,), (0,)), ((), ())), preferred_element_type=F32)


def mm_nt(a, b):
    return lax.dot_general(a, b, (((1,), (1,)), ((), ())), preferred_element_type=F32)


def kernel(c, order, x_ref, dy_ref, fac_ref, perm_ref, cho_ref, quota_ref, wg_hbm, wu_hbm, wd_hbm,
           mixed_ref, igrad_ref, coef_ref, *scratch):
    NX, NQ, NL, PC, J, Q, TOK = c.NX, c.NQ, c.NL, c.PC, c.J, c.Q, c.TOK
    NG, I, R, BL = c.NN, c.I, c.R, c.BL
    NI, NO = len(c.inp), len(c.out)
    refs = list(scratch)

    def take(n):
        return [refs.pop(0) for _ in range(n)]

    xg, zs, zr, ys, yr = [take(NI) for _ in range(5)]
    bs, br, rzs, rzr, part, rss, rsr = [take(NO) for _ in range(7)]
    (wg, wu, wd, pick, pickt, sel, selt, selg, ag, au, bk, hid, g_g, g_u, meta, m1, m2s, m2, cm, c1r, c2s, c2r, acat,
     pmask, cols_ref, w_sem, s_small, r_small, ag_s, ag_r, z_s, z_r, y_s, y_r, b_s, b_r, rz_s, rz_r, rs_s, rs_r) = refs
    LANES = 128
    node, y = lax.axis_index("node"), lax.axis_index("local")
    xx, b_me = lax.div(node, NQ), lax.rem(node, NQ)

    def x_peer(o):
        return lax.rem(xx + (o + NX), NX) * NQ + b_me

    def q_peer(i):
        q = lax.rem(b_me + i, NQ)
        return q, xx * NQ + q

    def y_peer(i):
        return lax.rem(y + i, NL)

    def copy(src, dst, send, recv, to_node, to_local):
        return pltpu.make_async_remote_copy(src_ref=src, dst_ref=dst, send_sem=send, recv_sem=recv,
                                            device_id=(to_node, to_local), device_id_type=MESH)

    def await_recv(like, sem):
        copy(like, like, sem, sem, node, y).wait_recv()

    def await_send(like, sem):
        copy(like, like, sem, sem, node, y).wait_send()

    barrier = pltpu.get_barrier_semaphore()
    for o in range(1, NX):
        pl.semaphore_signal(barrier, inc=1, device_id=(x_peer(o), y), device_id_type=MESH)
    for i in range(1, NQ):
        pl.semaphore_signal(barrier, inc=1, device_id=(q_peer(i)[1], y), device_id_type=MESH)
    for i in range(1, NL):
        pl.semaphore_signal(barrier, inc=1, device_id=(node, y_peer(i)), device_id_type=MESH)

    weights = [pltpu.make_async_copy(h.at[0], v, w_sem.at[n])
               for n, (h, v) in enumerate(((wg_hbm, wg), (wu_hbm, wu), (wd_hbm, wd)))]
    for w in weights:
        w.start()
    for s, (t, first, width) in enumerate(c.inp):
        xg[s][0] = (dy_ref if t else x_ref)[:, first:first + width]
    pl.semaphore_wait(barrier, (NX - 1) + (NQ - 1) + (NL - 1))

    rights, lefts = ring_steps(c)

    def offset_of(p):
        d = lax.shift_right_logical(p + 1, jnp.int32(1))
        return jnp.where((p & 1) == 1, -d, d)

    def static_offset(p):
        d = (p + 1) // 2
        return -d if p % 2 else d

    def do_ag(s, h):
        for side, steps in ((0, rights), (1, lefts)):
            if h >= 2 and (s, h - 2) not in waited:
                d0, h0 = steps[h - 2]
                await_recv(xg[s].at[slot_of(c, d0, side), pl.ds(h0 * c.H, c.H)], ag_r.at[s, side, h - 2])
            d, half = steps[h]
            rows = pl.ds(half * c.H, c.H)
            copy(xg[s].at[slot_of(c, d - 1, side), rows], xg[s].at[slot_of(c, d, side), rows],
                 ag_s.at[s], ag_r.at[s, side, h], x_peer(1 if side == 0 else -1), y).start()

    ag_seen = {s: 0 for s in range(NI)}

    def ag_upto(s, h):
        for g in range(ag_seen[s], h + 1):
            if g + 2 >= c.NH or (("ag", s, g + 2) not in issued):
                for side, steps in ((0, rights), (1, lefts)):
                    d0, h0 = steps[g]
                    await_recv(xg[s].at[slot_of(c, d0, side), pl.ds(h0 * c.H, c.H)], ag_r.at[s, side, g])
                waited.add((s, g))
        ag_seen[s] = max(ag_seen[s], h + 1)

    issued, waited = set(), set()

    def do_meta1():
        table = jnp.concatenate([v[...].astype(F32) for v in (cho_ref, fac_ref, perm_ref)], axis=0).astype(BF)
        eye = onehot(iota((TOK, TOK), 0) == iota((TOK, TOK), 1))
        turned = mm_nt(eye, table)
        cols_ref[...] = turned
        cho, perm = turned.astype(jnp.int32), turned[:, 2 * c.TOP:].astype(jnp.int32)
        fac = turned[:, c.TOP:2 * c.TOP]
        lane = iota((TOK, LANES), 1)
        code = iota((TOK, c.KG * NL), 1)
        table = jnp.zeros((TOK, c.KG * NL), F32)
        for n in range(c.TOP):
            table += jnp.where(cho[:, n:n + 1] == code, fac[:, n:n + 1], 0.0)
        table = table.astype(BF)
        groups = iota((TOK, NG), 1)
        named = []
        for s in range(c.KG):
            g = perm[:, s:s + 1]
            named.append(jnp.where(g == groups, 1.0, 0.0))
        total = sum(named[1:], named[0]).astype(BF)
        lower = onehot(iota((TOK, TOK), 1) < iota((TOK, TOK), 0))
        place = mm(lower, total)
        mark = (iota((TOK, LANES), 0) + 1).astype(F32)
        lane_j = idiv(lane, NL)
        out = jnp.zeros((NG, LANES), F32)
        eye = onehot(iota((NG, NG), 0) == iota((NG, NG), 1))
        for s in range(c.KG):
            p = jnp.sum(named[s] * place, axis=1, keepdims=True).astype(jnp.int32)
            spread = onehot((iota((c.KG * NL, LANES), 0) == s * NL + imod(iota((c.KG * NL, LANES), 1), NL)))
            mine = (lane_j == p) & (lane < J * NL)
            rhs = jnp.where(mine, mm(table, spread), 0.0)
            rhs += jnp.where(lane - J * NL == p, mark, 0.0)
            a = named[s].astype(BF)
            out += mm(mm_nt(eye, a).astype(BF), rhs.astype(BF))
            acat[s] = a
            pmask[s] = onehot(mine)
        meta[...] = out.reshape(NX, NQ, LANES)
        m1[0] = meta[xx]
        for p in range(1, NX):
            to = lax.rem(xx + (NX - static_offset(p)), NX)
            copy(meta.at[to], m1.at[p], s_small.at[0], r_small.at[0], to * NQ + b_me, y).start()

    def do_meta2():
        await_recv(m1.at[pl.ds(0, NX - 1)], r_small.at[0])
        flat = m1[...].reshape(NX * NQ, LANES).astype(BF)
        n = NX * NQ
        row, col = iota((n, n), 0), iota((n, n), 1)
        turn = onehot((imod(row, NX) == idiv(col, NQ)) & (idiv(row, NX) == imod(col, NQ)))
        m2s[...] = mm(turn, flat).reshape(NQ, NX, LANES)
        m2[b_me] = m2s[b_me]
        for i in range(1, NQ):
            q, to = q_peer(i)
            copy(m2s.at[q], m2.at[b_me], s_small.at[1], r_small.at[1], to, y).start()

    def do_pick():
        flat = m1[...].reshape(NX * NQ, LANES).astype(BF)
        C = NQ * BL
        row = iota((C, NX * NQ), 0)
        rq, rp = idiv(row, BL), idiv(imod(row, BL), J)
        lane, lrow = iota((C, LANES), 1), iota((C, LANES), 0)
        rcol = iota((C, 1), 0)
        ccol = iota((1, C), 1)
        for ch in range(2):
            take = onehot((rp + ch * PC) * NQ + rq == iota((C, NX * NQ), 1))
            got = jnp.where(lane == J * NL + imod(lrow, J), mm(take, flat), 0.0)
            down = jnp.sum(got, axis=1, keepdims=True).astype(jnp.int32)
            across = mm_nt(jnp.ones((8, LANES), BF), got.astype(BF))[0:1].astype(jnp.int32)
            down = jnp.where(down > 0, down + TOK * idiv(imod(rcol, BL), J), 0)
            across = jnp.where(across > 0, across + TOK * idiv(imod(ccol, BL), J), 0)
            pick[ch] = onehot(down == iota((C, PC * TOK), 1) + 1)
            pickt[ch] = onehot(across == iota((PC * TOK, C), 0) + 1)

    def slot_rows(v):
        half = NQ * BL
        ch = idiv(v, half)
        rest = v - ch * half
        return idiv(rest, BL) * NX + ch * PC + idiv(imod(rest, BL), J)

    def do_rank():
        await_recv(m2.at[pl.ds(0, NQ - 1)], r_small.at[1])
        n = NQ * NX
        mt = m2[...].reshape(n, LANES)
        lane = iota((n, LANES), 1)
        el = (mt != 0.0) & (lane < J * NL)
        elb = onehot(el)
        l0, l1 = iota((LANES, LANES), 0), iota((LANES, LANES), 1)
        same = (imod(l0, NL) == imod(l1, NL)) & (l0 < J * NL)
        inside = mm(elb, onehot(same & (idiv(l0, NL) < idiv(l1, NL))))
        rows = mm(elb, onehot(same)).astype(BF)

        def number(r):
            b, p = idiv(r, NX), imod(r, NX)
            return ((xx + offset_of(p) + NX) & (NX - 1)) * NQ + b

        before = onehot(number(iota((n, n), 1)) < number(iota((n, n), 0)))
        rank = inside + mm(before, rows)
        ql = jnp.broadcast_to(quota_ref[...].astype(F32), (8, NL)).astype(BF)
        ql = mm(ql, onehot(iota((NL, LANES), 0) == imod(iota((NL, LANES), 1), NL)))[0:1]
        keep = el & (rank < ql)
        rk = jnp.where(keep, rank + 1.0, 0.0).astype(BF)
        gk = jnp.where(keep, mt, 0.0).astype(BF)
        eye = onehot(l0 == l1)
        spread = onehot(iota((n, I), 0) == slot_rows(iota((n, I), 1)))
        mine = (idiv(iota((LANES, I), 0), NL) == imod(iota((LANES, I), 1), J)) & (iota((LANES, I), 0) < J * NL)
        fold = onehot((iota((max(NL, 8), LANES), 0) == imod(iota((max(NL, 8), LANES), 1), NL))
                      & (iota((max(NL, 8), LANES), 1) < J * NL))
        flat = jnp.where(mine, mm(mm_nt(eye, rk).astype(BF), spread), 0.0).astype(BF)
        flat = mm(fold, flat)
        for e in range(NL):
            sel[e] = onehot(flat[e:e + 1] == (iota((Q, I), 0) + 1).astype(F32))
        spread = onehot(slot_rows(iota((I, n), 0)) == iota((I, n), 1))
        mine = (idiv(iota((I, LANES), 1), NL) == imod(iota((I, LANES), 0), J)) & (iota((I, LANES), 1) < J * NL)
        widen = onehot((imod(iota((LANES, R), 0), NL) == idiv(iota((LANES, R), 1), Q)) & (iota((LANES, R), 0) < J * NL))
        flat = mm(jnp.where(mine, mm(spread, rk), 0.0).astype(BF), widen)
        gates = mm(jnp.where(mine, mm(spread, gk), 0.0).astype(BF), widen)
        hit = flat == (imod(iota((I, R), 1), Q) + 1).astype(F32)
        selt[...] = onehot(hit)
        selg[...] = jnp.where(hit, gates, 0.0).astype(BF)

    def do_z(s, ch):
        ag_upto(s, 3 if ch == 0 and c.D2 > 2 else c.NH - 1)
        width = c.inp[s][2]
        rows = xg[s][ch * PC:(ch + 1) * PC].reshape(PC * TOK, width)
        zs[s][ch] = mm(pick[ch], rows).astype(BF).reshape(NQ, BL, width)
        for i in far_first(NQ):
            q, to = q_peer(i)
            copy(zs[s].at[ch, q], zr[s].at[ch, b_me], z_s.at[s, ch], z_r.at[s, ch], to, y).start()
        zr[s][ch, b_me] = zs[s][ch, b_me]

    def do_y(s):
        width = c.inp[s][2]
        for ch in range(2):
            await_recv(zr[s].at[ch, pl.ds(0, NQ - 1)], z_r.at[s, ch])
        ys[s][...] = mm(sel[...].reshape(R, I), zr[s][...].reshape(I, width)).astype(BF).reshape(NL, Q, width)
        for i in far_first(NL):
            to = y_peer(i)
            copy(ys[s].at[to], yr[s].at[y], y_s.at[s], y_r.at[s], node, to).start()
        yr[s][y] = ys[s][y]

    def do_e(s):
        await_recv(yr[s].at[pl.ds(0, NL - 1)], y_r.at[s])
        t, first, width = c.inp[s]
        rows = yr[s][...].reshape(R, width)
        cols = slice(first, first + width)
        if s == 0:
            for w in weights:
                w.wait()
        if t == 0:
            a_g, a_u = mm(rows, wg[cols]), mm(rows, wu[cols])
            if first:
                a_g, a_u = a_g + ag[...], a_u + au[...]
            ag[...], au[...] = a_g, a_u
            if s == c.last[0]:
                hid[...] = (a_g * jax.nn.sigmoid(a_g) * a_u).astype(BF)
        else:
            back = mm_nt(rows, wd[:, cols])
            if first:
                back = back + bk[...]
            bk[...] = back
            if s == c.last[1]:
                a_g, a_u = ag[...], au[...]
                sig = jax.nn.sigmoid(a_g)
                g_g[...] = (back * a_u * sig * (1.0 + a_g * (1.0 - sig))).astype(BF)
                g_u[...] = (back * a_g * sig).astype(BF)

    def do_b(u):
        t, first, width = c.out[u]
        cols = slice(first, first + width)
        if t == 0:
            value = mm(hid[...], wd[:, cols])
        else:
            value = mm_nt(g_g[...], wg[cols]) + mm_nt(g_u[...], wu[cols])
        bs[u][...] = value.astype(BF).reshape(NL, Q, width)
        for i in far_first(NL):
            to = y_peer(i)
            copy(bs[u].at[to], br[u].at[y], b_s.at[u], b_r.at[u], node, to).start()
        br[u][y] = bs[u][y]

    b_seen = set()

    def do_m(u, ch):
        width = c.out[u][2]
        if u not in b_seen:
            b_seen.add(u)
            await_recv(br[u].at[pl.ds(0, NL - 1)], b_r.at[u])
        half = I // 2
        rzs[u][ch] = mm(selg[ch * half:(ch + 1) * half], br[u][...].reshape(R, width)).astype(BF).reshape(NQ, BL, width)
        for i in far_first(NQ):
            q, to = q_peer(i)
            copy(rzs[u].at[ch, q], rzr[u].at[ch, b_me], rz_s.at[u, ch], rz_r.at[u, ch], to, y).start()
        rzr[u][ch, b_me] = rzs[u][ch, b_me]

    def do_p(u, ch):
        width = c.out[u][2]
        await_recv(rzr[u].at[ch, pl.ds(0, NQ - 1)], rz_r.at[u, ch])
        sums = mm(pickt[ch], rzr[u][ch].reshape(NQ * BL, width))
        part[u][ch * PC:(ch + 1) * PC] = sums.reshape(PC, TOK, width)

    def do_rs(u, h):
        for side, steps in ((0, rights), (1, lefts)):
            d, half = steps[c.NH - 1 - h]
            value = part[u][slot_of(c, d, side), half * c.H:(half + 1) * c.H]
            if h >= 2:
                await_recv(rsr[u].at[side, h - 2], rs_r.at[u, side, h - 2])
                value = value + rsr[u][side, h - 2].astype(F32)
            rss[u][side, h] = value.astype(BF)
            copy(rss[u].at[side, h], rsr[u].at[side, h], rs_s.at[u, side], rs_r.at[u, side, h],
                 x_peer(-1 if side == 0 else 1), y).start()

    def do_fin(u):
        t, first, width = c.out[u]
        out = igrad_ref if t else mixed_ref
        values = [part[u][0, v * c.H:(v + 1) * c.H] for v in range(2)]
        for side, steps in ((0, rights), (1, lefts)):
            for h in (c.NH - 2, c.NH - 1):
                await_recv(rsr[u].at[side, h], rs_r.at[u, side, h])
                half = steps[c.NH - 1 - h][1]
                values[half] = values[half] + rsr[u][side, h].astype(F32)
        for v in range(2):
            out[v * c.H:(v + 1) * c.H, first:first + width] = values[v].astype(BF)

    def do_c1():
        cd = jnp.zeros((R, 1), F32)
        for s, (t, first, width) in enumerate(c.inp):
            for u, (v, begin, size) in enumerate(c.out):
                low, high = max(first, begin), min(first + width, begin + size)
                if t == 1 and v == 0 and low < high:
                    up = ys[s][:, :, low - first:high - first].reshape(R, high - low).astype(F32)
                    got = br[u][:, :, low - begin:high - begin].reshape(R, high - low).astype(F32)
                    cd += jnp.sum(up * got, axis=1, keepdims=True)
        spread = jnp.where(idiv(iota((R, LANES), 0), Q) == imod(iota((R, LANES), 1), NL), cd, 0.0).astype(BF)
        got = mm(selt[...], spread)
        mine = (idiv(iota((I, LANES), 1), NL) == imod(iota((I, LANES), 0), J)) & (iota((I, LANES), 1) < J * NL)
        got = jnp.where(mine, got, 0.0).astype(BF)
        n = NQ * NX
        fold = onehot(iota((n, I), 0) == slot_rows(iota((n, I), 1)))
        cm[...] = mm(fold, got).reshape(NQ, NX, LANES)
        c1r[b_me] = cm[b_me]
        for i in far_first(NQ):
            q, to = q_peer(i)
            copy(cm.at[q], c1r.at[b_me], s_small.at[2], r_small.at[2], to, y).start()

    def do_c2():
        await_recv(c1r.at[pl.ds(0, NQ - 1)], r_small.at[2])
        n = NX * NQ
        row, col = iota((n, n), 0), iota((n, n), 1)
        turn = onehot((imod(row, NQ) == idiv(col, NX)) & (idiv(row, NQ) == imod(col, NX)))
        c2s[...] = mm(turn, c1r[...].reshape(n, LANES).astype(BF)).reshape(NX, NQ, LANES)
        c2r[xx] = c2s[0]
        for p in range(1, NX):
            to = lax.rem(xx + (static_offset(p) + NX), NX)
            copy(c2s.at[p], c2r.at[xx], s_small.at[3], r_small.at[3], to * NQ + b_me, y).start()

    def do_c3():
        await_recv(c2r.at[pl.ds(0, NX - 1)], r_small.at[3])
        rows = c2r[...].reshape(NX * NQ, LANES).astype(BF)
        codes = c.KG * NL
        tab = jnp.zeros((TOK, codes), F32)
        for s in range(c.KG):
            mine = mm(acat[s], rows) * pmask[s].astype(F32)
            spread = onehot((iota((codes, LANES), 0) == s * NL + imod(iota((codes, LANES), 1), NL)))
            tab += mm_nt(mine.astype(BF), spread)
        cho = cols_ref[...].astype(jnp.int32)
        code, entry = iota((TOK, codes), 1), iota((TOK, c.TOP), 1)
        out = jnp.zeros((TOK, c.TOP), F32)
        for n in range(c.TOP):
            value = jnp.sum(jnp.where(cho[:, n:n + 1] == code, tab, 0.0), axis=1, keepdims=True)
            out += jnp.where(entry == n, value, 0.0)
        eye = onehot(iota((c.TOP, c.TOP), 0) == iota((c.TOP, c.TOP), 1))
        coef_ref[...] = mm_nt(eye, out.astype(BF)).astype(BF)

    steps = {"ag": do_ag, "z": do_z, "y": do_y, "e": do_e, "b": do_b, "m": do_m, "p": do_p, "rs": do_rs, "fin": do_fin,
             "meta1": do_meta1, "meta2": do_meta2, "pick": do_pick, "rank": do_rank,
             "c1": do_c1, "c2": do_c2, "c3": do_c3}
    for key in order:
        steps[key[0]](*key[1:])
        issued.add(key)

    for n, ref in enumerate((m1.at[pl.ds(0, NX - 1)], m2.at[pl.ds(0, NQ - 1)], c1r.at[pl.ds(0, NQ - 1)],
                             c2r.at[pl.ds(0, NX - 1)])):
        await_send(ref, s_small.at[n])
    for s in range(NI):
        await_send(xg[s].at[pl.ds(0, NX - 1)], ag_s.at[s])
        for ch in range(2):
            await_send(zs[s].at[ch, pl.ds(0, NQ - 1)], z_s.at[s, ch])
        await_send(ys[s].at[pl.ds(0, NL - 1)], y_s.at[s])
    for u in range(NO):
        for ch in range(2):
            await_send(rzs[u].at[ch, pl.ds(0, NQ - 1)], rz_s.at[u, ch])
        await_send(bs[u].at[pl.ds(0, NL - 1)], b_s.at[u])
        for side in range(2):
            await_send(rss[u].at[side], rs_s.at[u, side])


def per_device(c, x, dy, fac, perm, cho, quota, wg, wu, wd):
    NX, NQ, NL, PC, Q, TOK = c.NX, c.NQ, c.NL, c.PC, c.Q, c.TOK
    NI, NO = len(c.inp), len(c.out)
    order = ORDER if c.NX == 8 else plan(c)[0]
    dma = pltpu.SemaphoreType.DMA
    V = pltpu.VMEM
    C = NQ * c.BL
    scratch = []
    for lead, kind, streams in (
        ((NX, TOK), BF, c.inp), ((2, NQ, c.BL), BF, c.inp), ((2, NQ, c.BL), BF, c.inp), ((NL, Q), BF, c.inp), ((NL, Q), BF, c.inp),
        ((NL, Q), BF, c.out), ((NL, Q), BF, c.out), ((2, NQ, c.BL), BF, c.out), ((2, NQ, c.BL), BF, c.out),
        ((NX, TOK), F32, c.out), ((2, c.NH, c.H), BF, c.out), ((2, c.NH, c.H), BF, c.out),
    ):
        scratch += [V(lead + (width,), kind) for _, _, width in streams]
    scratch += [
        V((c.D, c.F), BF), V((c.D, c.F), BF), V((c.F, c.D), BF),
        V((2, C, PC * TOK), BF), V((2, PC * TOK, C), BF),
        V((NL, Q, c.I), BF), V((c.I, c.R), BF), V((c.I, c.R), BF),
        V((c.R, c.F), F32), V((c.R, c.F), F32), V((c.R, c.F), F32), V((c.R, c.F), BF), V((c.R, c.F), BF), V((c.R, c.F), BF),
        V((NX, NQ, 128), F32), V((NX, NQ, 128), F32), V((NQ, NX, 128), F32), V((NQ, NX, 128), F32),
        V((NQ, NX, 128), F32), V((NQ, NX, 128), F32), V((NX, NQ, 128), F32), V((NX, NQ, 128), F32),
        V((c.KG, TOK, c.NN), BF), V((c.KG, TOK, 128), BF), V((TOK, 2 * c.TOP + c.KG), F32),
        dma((3,)), dma((4,)), dma((4,)),
        dma((NI,)), dma((NI, 2, c.NH)), dma((NI, 2)), dma((NI, 2)), dma((NI,)), dma((NI,)),
        dma((NO,)), dma((NO,)), dma((NO, 2)), dma((NO, 2)), dma((NO, 2)), dma((NO, 2, c.NH)),
    ]
    vm = pl.BlockSpec(memory_space=pltpu.VMEM)
    hbm = pl.BlockSpec(memory_space=pl.ANY)
    flops = 2 * c.R * c.D * c.F * 6
    mixed, grads, coef = pl.pallas_call(
        functools.partial(kernel, c, order),
        out_shape=(jax.ShapeDtypeStruct((TOK, c.D), BF), jax.ShapeDtypeStruct((TOK, c.D), BF),
                   jax.ShapeDtypeStruct((c.TOP, TOK), BF)),
        in_specs=[vm] * 6 + [hbm] * 3,
        out_specs=(vm, vm, vm),
        scratch_shapes=scratch,
        compiler_params=pltpu.CompilerParams(collective_id=0, has_side_effects=True, vmem_limit_bytes=60 * 2**20),
        cost_estimate=pl.CostEstimate(flops=flops, bytes_accessed=4 * 2**20, transcendentals=c.R * c.F),
        name="expert_layer",
    )(x, dy, fac.T, perm.T, cho.T, quota.reshape(1, NL), wg, wu, wd)
    return mixed, grads, coef.T


def solution(mesh, **over):
    def step(x, dy, fac, perm, cho, quota, wg, wu, wd):
        c = config(mesh, x.shape[0], perm.shape[1], cho.shape[1], x.shape[1], wg.shape[2], **over)
        return per_device(c, x, dy, fac, perm, cho, quota, wg, wu, wd)

    rows = P(("node", "local"), None)
    cube = P(("node", "local"), None, None)
    return jax.shard_map(
        step,
        mesh=mesh,
        in_specs=(rows, rows, rows, rows, rows, P("node"), cube, cube, cube),
        out_specs=(rows, rows, rows),
        check_vma=False,
    )
```
